32 devices in a mesh: expert: 4 (over z), ctx: 4 (over x, core), dp: 2 (over y).
Axes of the slice: x: 2, y: 2, z: 4, core: 2. Of those that a mesh axis runs over, the one named last changes fastest.
Arguments:
- inputs: bfloat16 [4, 1024, 768], P('expert', ('ctx', 'dp')), may hold values from -6 to 6
- cotangent: bfloat16 [4, 1024, 768], P('expert', ('ctx', 'dp')), may hold values from -6 to 6
- expert_ids: int32 [4, 1024, 2], P('expert', ('ctx', 'dp')), may hold values from 0 to 3, all different within a row; in each aligned block of 128 rows (0 to 127, 128 to 255, ..., all dimensions but the last counted through in order) at most 72 rows name the same one
- first_gain: float32 [768], replicated, may hold values from 0.1 to 1.9
- query_weight: bfloat16 [768, 768], replicated, may hold values from -0.21875 to 0.21875
- key_weight: bfloat16 [768, 768], replicated, may hold values from -0.21875 to 0.21875
- value_weight: bfloat16 [768, 768], replicated, may hold values from -0.21875 to 0.21875
- merge_weight: bfloat16 [768, 768], replicated, may hold values from -0.875 to 0.875
- relative_bucket_bias: float32 [32, 12], replicated, may hold values from -4 to 4
- expert_norm_gain: float32 [768], replicated, may hold values from 0.1 to 1.9
- router_weight: bfloat16 [768, 4], replicated, may hold values from -0.15625 to 0.15625
- gate_weight: bfloat16 [4, 768, 3072], P('expert', None, 'ctx'), may hold values from -0.21875 to 0.21875
- up_weight: bfloat16 [4, 768, 3072], P('expert', None, 'ctx'), may hold values from -0.21875 to 0.21875
- down_weight: bfloat16 [4, 3072, 768], P('expert', 'ctx'), may hold values from -0.109375 to 0.109375
Outputs:
- layer_output: bfloat16 [4, 1024, 768], P('expert', ('ctx', 'dp'))
- input_grad: float32 [4, 1024, 768], P('expert', ('ctx', 'dp'))
- first_grad: float32 [768], replicated
- query_grad: float32 [768, 768], P(('ctx', 'dp'), 'expert')
- key_grad: float32 [768, 768], P(('ctx', 'dp'), 'expert')
- value_grad: float32 [768, 768], P(('ctx', 'dp'), 'expert')
- merge_grad: float32 [768, 768], P(('ctx', 'dp'), 'expert')
- bias_grad: float32 [32, 12], replicated
- second_grad: float32 [768], replicated
- router_grad: float32 [768, 4], replicated
- gate_grad: float32 [4, 768, 3072], P('expert', 'dp', 'ctx')
- up_grad: float32 [4, 768, 3072], P('expert', 'dp', 'ctx')
- down_grad: float32 [4, 3072, 768], P('expert', 'ctx', 'dp')
The draws below stay inside these ranges and needn't reach their ends.
Inputs may be any that keep to these rules, and one draw needn't show every extreme that they name: `expert_ids`: A token's two experts differ. In each sequence, the 128 positions of an aligned block name any one expert at most 72 times, and in every draw some expert is named exactly 72 times in some block.
All inputs are finite; a program needn't handle non-finite values.
Results may differ from the reference program's by a relative error of at most 0.017.
Values may be sent and summed in bfloat16 or wider, within the bound.
A program may use at most 192 MiB of HBM per device.

```python
import math
import jax
import jax.numpy as jnp
import numpy as np
from jax import lax

D = 768
HEADS = 12
HEAD_DIM = 64
FF = 3072
BUCKETS = 32
POS_DEV = 128
EXPERTS = 4
CAP = 72
SEQ_LEN = 1024
SEQS = 4


def level_of(own_key, dims, shards, smallest, high):
    factor_of, own = 1.0, jax.random.fold_in(own_key, 6)
    for position, blocks in shards:
        heights = jnp.exp(jax.random.uniform(jax.random.fold_in(own, position), (blocks,), jnp.float32, smallest / len(shards), high / len(shards)))
        factor_of = factor_of * jnp.repeat(heights, dims[position] // blocks).reshape([-1 if axis == position else 1 for axis in range(len(dims))])
    return factor_of


def deal_out(key, own, number, rows, number_of, top, reach, slope):
    order = jax.random.permutation(key, number_of)
    heavy_load, usual = portions_of(number_of, rows * top, reach, slope, True), portions_of(number_of, rows * top, reach, slope, False)
    places = jnp.arange(number_of)

    def named(tallies, rotation):
        used = int((tallies > 0).sum())
        fixed = max(1, used // 4)
        passed = fixed + (places - fixed + rotation * (used - fixed)) % max(1, number_of - fixed)
        return jnp.zeros((number_of,), jnp.int32).at[order[jnp.where(places < fixed, places, passed)]].set(jnp.asarray(tallies, jnp.int32))

    tallies = jnp.where(number % 4 == 0, named(heavy_load, number // 4), named(usual, number - number // 4 - 1))
    mixed = jax.random.permutation(jax.random.fold_in(own, 3), number_of)
    donor, receiver = mixed[0:number_of // 2 * 2:2], mixed[1:number_of // 2 * 2:2]
    slack = jnp.minimum(tallies[donor] - 1, reach - tallies[receiver]) // 2
    slack = jnp.where((donor == order[0]) | (receiver == order[0]) | (tallies[receiver] == 0), 0, jnp.maximum(slack, 0))
    passed = jax.random.randint(jax.random.fold_in(own, 4), (number_of // 2,), 0, 1 << 20) % (slack + 1)
    tallies = tallies.at[donor].add(-passed).at[receiver].add(passed)
    items = jnp.searchsorted(jnp.cumsum(tallies), jnp.arange(rows * top), side="right").astype(jnp.int32)
    listing = items.reshape(top, rows).T
    listing = listing[jax.random.permutation(jax.random.fold_in(own, 1), rows)]
    rotation = jax.random.randint(jax.random.fold_in(own, 2), (rows, 1), 0, top)
    return jnp.take_along_axis(listing, (jnp.arange(top)[None, :] + rotation) % top, axis=1)


def portions_of(count, total, bound, skew, full):
    loads = [(1 << 20) // math.isqrt(rank ** skew) + 1 for rank in range(1, count + 1)]
    largest = bound if full else min(bound, max(-(-total // count), total * loads[0] // sum(loads)))
    least = 1 if total - largest >= count - 1 else 0
    given, surplus = [largest] + [least] * (count - 1), total - largest - least * (count - 1)
    while surplus > 0:
        movable = [i for i in range(1, count) if given[i] < largest] or [i for i in range(1, count) if given[i] < bound]
        pool, remaining = sum([loads[i] for i in movable]), surplus
        for i in movable:
            more = min(bound - given[i], max(1, remaining * loads[i] // pool), surplus)
            given[i] = given[i] + more
            surplus = surplus - more
    return np.array(given)


def bell_draw(own_key, extent, spread, limit, shards=(), held_as=jnp.bfloat16):
    array = jax.random.normal(own_key, extent, jnp.float32) * spread
    if len(shards) > 0:
        array = level_of(own_key, extent, shards, -0.22, 0.18) * array
    return jnp.clip(array, min=-limit, max=limit).astype(held_as)


def setup_inputs(seed: int = 0) -> dict:
    keys = jax.random.split(jax.random.key(seed), 15)
    inputs = bell_draw(keys[0], (SEQS, SEQ_LEN, D), 1.0, 6.0, ((0, 4), (1, 8)))
    cotangent = bell_draw(keys[1], (SEQS, SEQ_LEN, D), 1.0, 6.0, ((0, 4), (1, 8)))
    expert_ids_keys = jax.random.split(jax.random.fold_in(keys[2], 1), SEQS * SEQ_LEN // POS_DEV)
    expert_ids_turns = jax.random.permutation(jax.random.fold_in(keys[2], 3), SEQS * SEQ_LEN // POS_DEV)
    expert_ids = jax.vmap(lambda own, number: deal_out(jax.random.fold_in(keys[2], 2), own, number, POS_DEV, EXPERTS, 2, CAP, 1))(expert_ids_keys, expert_ids_turns).reshape((SEQS, SEQ_LEN, 2))
    first_gain = jnp.clip(1.0 + 0.18 * jax.random.normal(keys[3], (D,), jnp.float32), 0.1, 1.9)
    query_weight = bell_draw(keys[4], (D, D), D ** -0.5, 0.21875)
    key_weight = bell_draw(keys[5], (D, D), D ** -0.5, 0.21875)
    value_weight = bell_draw(keys[6], (D, D), D ** -0.5, 0.21875)
    merge_weight = bell_draw(keys[7], (D, D), (D // 16) ** -0.5, 0.875)
    relative_bucket_bias = bell_draw(keys[8], (BUCKETS, HEADS), 1.0, 4.0, (), jnp.float32)
    expert_norm_gain = jnp.clip(1.0 + 0.18 * jax.random.normal(keys[9], (D,), jnp.float32), 0.1, 1.9)
    router_weight = bell_draw(keys[10], (D, EXPERTS), (2 * D) ** -0.5, 0.15625)
    gate_weight = bell_draw(keys[11], (EXPERTS, D, FF), D ** -0.5, 0.21875, ((0, 4), (2, 4)))
    up_weight = bell_draw(keys[12], (EXPERTS, D, FF), D ** -0.5, 0.21875, ((0, 4), (2, 4)))
    down_weight = bell_draw(keys[13], (EXPERTS, FF, D), FF ** -0.5, 0.109375, ((0, 4), (1, 4)))
    return {"inputs": inputs, "cotangent": cotangent, "expert_ids": expert_ids, "first_gain": first_gain, "query_weight": query_weight, "key_weight": key_weight, "value_weight": value_weight, "merge_weight": merge_weight, "relative_bucket_bias": relative_bucket_bias, "expert_norm_gain": expert_norm_gain, "router_weight": router_weight, "gate_weight": gate_weight, "up_weight": up_weight, "down_weight": down_weight}


norm_eps = 1e-06
reach_span = 128.0

@jax.custom_vjp
def low(v):
    return lax.optimization_barrier(v.astype(jnp.bfloat16)).astype(jnp.float32)

@jax.custom_vjp
def low_back(v):
    return v

def low_keep(v):
    return (low(v), None)

def low_pass(kept, grad):
    return (grad,)

def back_keep(v):
    return (v, None)

def back_low(kept, grad):
    return (low(grad),)
low.defvjp(low_keep, low_pass)
low_back.defvjp(back_keep, back_low)

def bucket_bounds(bucket_num):
    exact_span = bucket_num // 2
    bounds = list(range(1, exact_span))
    for target in range(exact_span, bucket_num):
        border = exact_span
        while exact_span + int(math.log(border / exact_span) / math.log(reach_span / exact_span) * exact_span) < target:
            border += 1
        bounds.append(border)
    return bounds

def distance_buckets(distance, bucket_num):
    counted = jnp.zeros(distance.shape, jnp.int32)
    for border in bucket_bounds(bucket_num):
        counted = counted + (distance >= border).astype(jnp.int32)
    return counted

def rms_scale(values, gain_vec):
    return values * lax.rsqrt(lax.optimization_barrier(jnp.mean(values * values, axis=-1, keepdims=True)) + norm_eps) * gain_vec

def attend_one(query_seq, key_seq, value_seq, bias_lattice, visible):
    highest_precision = lax.Precision.HIGHEST
    raw_scores = jnp.einsum('qhd,khd->hqk', query_seq, key_seq, precision=highest_precision, preferred_element_type=jnp.float32) * HEAD_DIM ** (-0.5) + bias_lattice
    raw_scores = low_back(raw_scores)
    masked = jnp.where(visible[None], raw_scores, -1e+30)
    row_top = lax.optimization_barrier(jnp.max(masked, axis=-1, keepdims=True))
    exp_terms = jnp.exp(masked - row_top)
    prob_mass = exp_terms / lax.optimization_barrier(jnp.sum(exp_terms, axis=-1, keepdims=True))
    return jnp.einsum('hqk,khd->qhd', low(prob_mass), value_seq, precision=highest_precision, preferred_element_type=jnp.float32)

def expert_one(pieces):
    slot_rows, gate_matrix, up_matrix, down_matrix = pieces
    highest_precision = lax.Precision.HIGHEST
    gate_pre = low_back(jnp.dot(slot_rows, gate_matrix, precision=highest_precision, preferred_element_type=jnp.float32))
    up_pre = low_back(jnp.dot(slot_rows, up_matrix, precision=highest_precision, preferred_element_type=jnp.float32))
    hidden = low(jax.nn.gelu(gate_pre, approximate=False) * up_pre)
    return low_back(low(jnp.dot(hidden, down_matrix, precision=highest_precision, preferred_element_type=jnp.float32)))

def reference(inputs, cotangent, expert_ids, first_gain, query_weight, key_weight, value_weight, merge_weight, relative_bucket_bias, expert_norm_gain, router_weight, gate_weight, up_weight, down_weight):
    highest_precision = lax.Precision.HIGHEST
    positions = jnp.arange(SEQ_LEN, dtype=jnp.int32)
    offsets = positions[:, None] - positions[None, :]
    visible = offsets >= 0
    buckets = distance_buckets(jnp.clip(offsets, 0, SEQ_LEN - 1), BUCKETS)
    block_count = SEQS * (SEQ_LEN // POS_DEV)
    assign_ids = expert_ids.reshape(block_count, POS_DEV * 2)
    expert_hot = (assign_ids[:, :, None] == jnp.arange(EXPERTS, dtype=jnp.int32)[None, None, :]).astype(jnp.int32)
    earlier = (jnp.cumsum(expert_hot, axis=1) - expert_hot).astype(jnp.int32)
    slot_pos = lax.optimization_barrier(jnp.sum(earlier * expert_hot, axis=-1)).astype(jnp.int32)
    buffer_row = (jnp.arange(block_count, dtype=jnp.int32)[:, None] * CAP + slot_pos).reshape(-1).astype(jnp.int32)
    routed_flat = expert_ids.reshape(-1).astype(jnp.int32)
    buffer_len = block_count * CAP
    head_shape = (SEQS, SEQ_LEN, HEADS, HEAD_DIM)

    def forward(residual, first_gain, query_weight, key_weight, value_weight, merge_weight, relative_bucket_bias, expert_norm_gain, router_weight, gate_weight, up_weight, down_weight):
        mixer_in = low(rms_scale(residual, first_gain))
        queries = low_back(low(jnp.einsum('spd,de->spe', mixer_in, query_weight, precision=highest_precision, preferred_element_type=jnp.float32)))
        keys_all = low_back(low(jnp.einsum('spd,de->spe', mixer_in, key_weight, precision=highest_precision, preferred_element_type=jnp.float32)))
        values = low_back(low(jnp.einsum('spd,de->spe', mixer_in, value_weight, precision=highest_precision, preferred_element_type=jnp.float32)))
        bias_lattice = jnp.take(relative_bucket_bias, buckets, axis=0).transpose(2, 0, 1)
        run_one = jax.checkpoint(attend_one)

        def by_sequence(pieces):
            return run_one(pieces[0], pieces[1], pieces[2], bias_lattice, visible)
        attended = lax.map(by_sequence, (queries.reshape(head_shape), keys_all.reshape(head_shape), values.reshape(head_shape)))
        mixed_heads = low_back(low(attended.reshape(SEQS, SEQ_LEN, D)))
        hidden_state = residual + low_back(jnp.einsum('spd,de->spe', mixed_heads, merge_weight, precision=highest_precision, preferred_element_type=jnp.float32))
        expert_input = low(rms_scale(hidden_state, expert_norm_gain)).reshape(SEQS * SEQ_LEN, D)
        logits = low_back(jnp.dot(expert_input, router_weight, precision=highest_precision, preferred_element_type=jnp.float32))
        routed_ids = expert_ids.reshape(SEQS * SEQ_LEN, 2)
        gate_values = jax.nn.softmax(jnp.take_along_axis(logits, routed_ids, axis=1), axis=-1)
        packed = jnp.zeros((EXPERTS, buffer_len, D), jnp.float32).at[routed_flat, buffer_row].set(jnp.repeat(expert_input, 2, axis=0))
        packed = low_back(packed)
        results = lax.map(jax.checkpoint(expert_one), (packed, gate_weight, up_weight, down_weight))
        picked = results[routed_flat, buffer_row].reshape(SEQS * SEQ_LEN, 2, D)
        expert_sum = lax.optimization_barrier(jnp.sum(gate_values[:, :, None] * picked, axis=1))
        return hidden_state + expert_sum.reshape(SEQS, SEQ_LEN, D)
    layer_output, pullback = jax.vjp(forward, inputs.astype(jnp.float32), first_gain.astype(jnp.float32), query_weight.astype(jnp.float32), key_weight.astype(jnp.float32), value_weight.astype(jnp.float32), merge_weight.astype(jnp.float32), relative_bucket_bias.astype(jnp.float32), expert_norm_gain.astype(jnp.float32), router_weight.astype(jnp.float32), gate_weight.astype(jnp.float32), up_weight.astype(jnp.float32), down_weight.astype(jnp.float32))
    gradients = pullback(cotangent.astype(jnp.float32))
    return (layer_output.astype(jnp.bfloat16), gradients[0], gradients[1], gradients[2], gradients[3], gradients[4], gradients[5], gradients[6], gradients[7], gradients[8], gradients[9], gradients[10], gradients[11])
```

```python
import math

import jax
import jax.numpy as jnp
from jax import lax
from jax.sharding import PartitionSpec as P

norm_eps = 1e-06
reach_span = 128.0


def bucket_bounds(bucket_num):
    exact_span = bucket_num // 2
    bounds = list(range(1, exact_span))
    for target in range(exact_span, bucket_num):
        border = exact_span
        while (
            exact_span
            + int(math.log(border / exact_span) / math.log(reach_span / exact_span) * exact_span)
            < target
        ):
            border += 1
        bounds.append(border)
    return bounds


def distance_buckets(distance, bucket_num):
    counted = jnp.zeros(distance.shape, jnp.int32)
    for border in bucket_bounds(bucket_num):
        counted = counted + (distance >= border).astype(jnp.int32)
    return counted


def rms_scale(values, gain_vec):
    return (
        values * lax.rsqrt(jnp.mean(values * values, axis=-1, keepdims=True) + norm_eps) * gain_vec
    )


def gated_hidden(gate_pre, up_pre):
    return jax.nn.gelu(gate_pre, approximate=False) * up_pre


def pair_softmax(logit_pair):
    return jax.nn.softmax(logit_pair, axis=-1)


def bucket_table(distance, bucket_num):
    bucket_of = distance_buckets(distance, bucket_num)
    return (lax.iota(jnp.int32, bucket_num)[:, None, None] == bucket_of[None]).astype(jnp.float32)


def split_parts(values, count):
    parts = []
    rest = values
    for _ in range(count):
        part = rest.astype(jnp.bfloat16)
        parts.append(part)
        rest = rest - part.astype(jnp.float32)
    return parts


def bias_grid(bias_table, distance):
    bucket_num = bias_table.shape[0]
    hot = bucket_table(distance, bucket_num).astype(jnp.bfloat16)
    table = jnp.concatenate(split_parts(bias_table, 3), axis=0)
    return jnp.einsum(
        "ry,rta->yta",
        table,
        jnp.concatenate([hot, hot, hot], axis=0),
        preferred_element_type=jnp.float32,
    )


def slot_hot(hits, capacity):
    pos_count = hits.shape[-1]
    before = (
        lax.iota(jnp.int32, pos_count)[:, None] < lax.iota(jnp.int32, pos_count)[None, :]
    ).astype(jnp.bfloat16)
    slots = jnp.einsum(
        "...p,pq->...q", hits.astype(jnp.bfloat16), before, preferred_element_type=jnp.float32
    ).astype(jnp.int32)
    rows = lax.iota(jnp.int32, capacity)[:, None]
    return jnp.where(
        hits[..., None, :] & (slots[..., None, :] == rows), 1.0, 0.0
    ).astype(jnp.bfloat16)


def total_over(values, axes):
    flat = jnp.concatenate([value.reshape(-1) for value in values])
    size = flat.shape[0]
    pad = (-size) % 1024
    packed = jnp.pad(flat, (0, pad)).reshape(1, -1, 128)
    summed = jnp.sum(lax.all_gather(packed, axes, axis=0, tiled=True), axis=0).reshape(-1)
    outs = []
    offset = 0
    for value in values:
        outs.append(summed[offset : offset + value.size].reshape(value.shape))
        offset += value.size
    return outs


def per_device(
    inputs,
    cotangent,
    expert_ids,
    first_gain,
    query_weight,
    key_weight,
    value_weight,
    merge_weight,
    relative_bucket_bias,
    expert_norm_gain,
    router_weight,
    gate_weight,
    up_weight,
    down_weight,
):
    seq_count, pos_count, model_width = inputs.shape
    bucket_num, heads_num = relative_bucket_bias.shape
    head_dimension = model_width // heads_num
    score_scale = head_dimension ** (-0.5)
    expert_num = router_weight.shape[1]
    local_experts = gate_weight.shape[0]
    owners = lax.axis_size("expert")
    places = lax.axis_size(("ctx", "dp"))
    seq_len = pos_count * places
    capacity = min(pos_count, max(2, 9 * pos_count // (4 * expert_num)))
    lane_rows = seq_count * capacity
    everyone = ("expert", "ctx", "dp")
    column_count = model_width // owners
    first_expert = lax.axis_index("expert") * local_experts
    ids_all = lax.all_gather(expert_ids, ("ctx", "expert"), axis=0, tiled=True)
    block_num = ids_all.shape[0]
    residual = inputs.astype(jnp.float32)
    first_normed, first_back = jax.vjp(rms_scale, residual, first_gain)
    mixer_in = first_normed.astype(jnp.bfloat16)
    keys_local = jnp.einsum(
        "spd,de->spe", mixer_in, key_weight, preferred_element_type=jnp.float32
    ).astype(jnp.bfloat16)
    values_local = jnp.einsum(
        "spd,de->spe", mixer_in, value_weight, preferred_element_type=jnp.float32
    ).astype(jnp.bfloat16)
    keys_whole, values_whole = (
        lax.all_gather(keys_local, ("ctx", "dp"), axis=1, tiled=True),
        lax.all_gather(values_local, ("ctx", "dp"), axis=1, tiled=True),
    )
    queries = jnp.einsum(
        "spd,de->spe", mixer_in, query_weight, preferred_element_type=jnp.float32
    ).astype(jnp.bfloat16)
    query_heads = queries.reshape(seq_count, pos_count, heads_num, head_dimension)
    key_heads = keys_whole.reshape(seq_count, seq_len, heads_num, head_dimension)
    value_heads = values_whole.reshape(seq_count, seq_len, heads_num, head_dimension)
    first_pos = lax.axis_index(("ctx", "dp")) * pos_count
    query_pos = first_pos + lax.iota(jnp.int32, pos_count)
    offsets = query_pos[:, None] - lax.iota(jnp.int32, seq_len)[None, :]
    visible = offsets >= 0
    distance = jnp.clip(offsets, 0, seq_len - 1)
    bias_lattice = bias_grid(relative_bucket_bias, distance)
    raw_scores = (
        jnp.einsum("sqhd,skhd->shqk", query_heads, key_heads, preferred_element_type=jnp.float32)
        * score_scale
        + bias_lattice[None]
    )
    masked = jnp.where(visible[None, None], raw_scores, -1e30)
    row_top = jnp.max(masked, axis=-1, keepdims=True)
    exp_terms = jnp.exp(masked - row_top)
    row_total = jnp.sum(exp_terms, axis=-1, keepdims=True)
    prob_mass = exp_terms / row_total
    log_total = row_top + jnp.log(row_total)
    attended = jnp.einsum(
        "shqk,skhd->sqhd",
        prob_mass.astype(jnp.bfloat16),
        value_heads,
        preferred_element_type=jnp.float32,
    )
    total_rows = log_total[..., 0].transpose(0, 2, 1)
    stat_pad = -(-3 * heads_num // 128) * 128 - 3 * heads_num
    stat_zeros = jnp.zeros((seq_count, pos_count, stat_pad), jnp.bfloat16)
    query_packed = jnp.concatenate([queries, *split_parts(total_rows, 3), stat_zeros], axis=-1)
    cotangent_free, values_whole = lax.optimization_barrier((cotangent, values_whole))
    cotangent_all = lax.all_gather(cotangent_free, ("ctx", "expert"), axis=0, tiled=True)
    mixer_all = lax.all_gather(mixer_in, "expert", axis=0, tiled=True)
    mixed_heads = attended.reshape(seq_count, pos_count, model_width).astype(jnp.bfloat16)
    hidden_state = residual + jnp.einsum(
        "spd,de->spe", mixed_heads, merge_weight, preferred_element_type=jnp.float32
    )
    second_normed, second_back = jax.vjp(rms_scale, hidden_state, expert_norm_gain)
    expert_input = second_normed.astype(jnp.bfloat16)
    own_hits = jnp.any(
        expert_ids[None] == lax.iota(jnp.int32, expert_num)[:, None, None, None], axis=-1
    )
    own_hot = slot_hot(own_hits, capacity)
    dispatched = (
        jnp.einsum("eskp,spd->eskd", own_hot, expert_input, preferred_element_type=jnp.float32)
        .astype(jnp.bfloat16)
        .reshape(owners, local_experts, lane_rows, model_width)
    )
    arrived = lax.all_to_all(dispatched, "expert", split_axis=0, concat_axis=0, tiled=True)
    slot_rows = arrived.transpose(1, 0, 2, 3).reshape(
        local_experts, owners * lane_rows, model_width
    )
    all_rows = lax.all_gather(slot_rows, "ctx", axis=1, tiled=True)
    my_experts = first_expert + lax.iota(jnp.int32, local_experts)
    block_hits = jnp.any(ids_all[None] == my_experts[:, None, None, None], axis=-1)
    block_hot = slot_hot(block_hits, capacity)
    other_ids = jnp.sum(ids_all, axis=-1)[None] - my_experts[:, None, None]
    row_other = jnp.sum(
        block_hot.astype(jnp.float32) * other_ids[:, :, None, :].astype(jnp.float32), axis=-1
    ).astype(jnp.int32).reshape(local_experts, block_num * capacity)
    cotangent_rows = jnp.einsum(
        "lbkp,bpd->lbkd", block_hot, cotangent_all, preferred_element_type=jnp.float32
    ).astype(jnp.bfloat16).reshape(local_experts, block_num * capacity, model_width)
    row_logits = jnp.einsum(
        "lrd,de->lre", all_rows, router_weight, preferred_element_type=jnp.float32
    )
    expert_line = lax.iota(jnp.int32, expert_num)[None, None, :]
    own_logit = jnp.sum(
        jnp.where(expert_line == my_experts[:, None, None], row_logits, 0.0), axis=-1
    )
    other_logit = jnp.sum(jnp.where(expert_line == row_other[..., None], row_logits, 0.0), axis=-1)
    row_gates = jax.nn.sigmoid(own_logit - other_logit)
    all_grads = (row_gates[..., None] * cotangent_rows.astype(jnp.float32)).astype(jnp.bfloat16)
    gate_pre = jnp.einsum("erd,edf->erf", all_rows, gate_weight, preferred_element_type=jnp.float32)
    up_pre = jnp.einsum("erd,edf->erf", all_rows, up_weight, preferred_element_type=jnp.float32)
    hidden_float, act_back = jax.vjp(gated_hidden, gate_pre, up_pre)
    hidden_act = hidden_float.astype(jnp.bfloat16)
    partial_value = jnp.einsum(
        "erf,efd->erd", hidden_act, down_weight, preferred_element_type=jnp.float32
    ).astype(jnp.bfloat16)
    partial_value, all_grads = lax.optimization_barrier((partial_value, all_grads))
    expert_result = lax.psum_scatter(partial_value, "ctx", scatter_dimension=1, tiled=True)
    returning = expert_result.reshape(local_experts, owners, lane_rows, model_width).transpose(
        1, 0, 2, 3
    )
    returned = lax.all_to_all(returning, "expert", split_axis=0, concat_axis=0, tiled=True)
    hidden_grad = jnp.einsum(
        "erd,efd->erf", all_grads, down_weight, preferred_element_type=jnp.float32
    )
    gate_delta, up_delta = act_back(hidden_grad)
    gate_low = gate_delta.astype(jnp.bfloat16)
    up_low = up_delta.astype(jnp.bfloat16)
    row_part = (
        jnp.einsum("erf,edf->erd", gate_low, gate_weight, preferred_element_type=jnp.float32)
        + jnp.einsum("erf,edf->erd", up_low, up_weight, preferred_element_type=jnp.float32)
    ).astype(jnp.bfloat16)
    row_grads = lax.psum_scatter(row_part, "ctx", scatter_dimension=1, tiled=True)
    back_rows = row_grads.reshape(local_experts, owners, lane_rows, model_width).transpose(
        1, 0, 2, 3
    )
    returned_grads = lax.all_to_all(back_rows, "expert", split_axis=0, concat_axis=0, tiled=True)
    mixed_all = lax.all_gather(mixed_heads, "expert", axis=0, tiled=True)
    query_whole = lax.all_gather(query_packed, ("ctx", "dp"), axis=1, tiled=True)
    down_part = jnp.einsum(
        "erf,erd->efd", hidden_act, all_grads, preferred_element_type=jnp.float32
    )
    gate_part = jnp.einsum("erd,erf->edf", all_rows, gate_low, preferred_element_type=jnp.float32)
    up_part = jnp.einsum("erd,erf->edf", all_rows, up_low, preferred_element_type=jnp.float32)
    gate_grad, up_grad, down_grad = (
        lax.psum_scatter(
            gate_part.astype(jnp.bfloat16), "dp", scatter_dimension=1, tiled=True
        ).astype(jnp.float32),
        lax.psum_scatter(
            up_part.astype(jnp.bfloat16), "dp", scatter_dimension=1, tiled=True
        ).astype(jnp.float32),
        lax.psum_scatter(
            down_part.astype(jnp.bfloat16), "dp", scatter_dimension=2, tiled=True
        ).astype(jnp.float32),
    )
    logits = jnp.einsum(
        "spd,de->spe", expert_input, router_weight, preferred_element_type=jnp.float32
    )
    pick_hot = expert_ids[..., None] == lax.iota(jnp.int32, expert_num)
    picked_logits = jnp.sum(jnp.where(pick_hot, logits[:, :, None, :], 0.0), axis=-1)
    gate_values, gate_back = jax.vjp(pair_softmax, picked_logits)
    upstream = cotangent.astype(jnp.float32)
    slot_table = own_hot.transpose(1, 0, 2, 3)
    choose = (
        slot_table[:, None] * pick_hot.transpose(0, 2, 3, 1)[:, :, :, None, :].astype(jnp.bfloat16)
    ).reshape(seq_count, 2, expert_num * capacity, pos_count)
    returned_rows = returned.reshape(expert_num, seq_count, capacity, model_width).transpose(
        1, 0, 2, 3
    ).reshape(seq_count, expert_num * capacity, model_width)
    picked = jnp.einsum(
        "sjmp,smd->sjpd", choose, returned_rows, preferred_element_type=jnp.float32
    )
    expert_sum = (
        gate_values[:, :, 0, None] * picked[:, 0] + gate_values[:, :, 1, None] * picked[:, 1]
    )
    layer_output = (hidden_state + expert_sum).astype(jnp.bfloat16)
    pair_delta = jnp.sum(upstream[:, None] * picked, axis=-1).transpose(0, 2, 1)
    (pick_grad,) = gate_back(pair_delta)
    logit_grad = jnp.sum(jnp.where(pick_hot, pick_grad[..., None], 0.0), axis=2).astype(
        jnp.bfloat16
    )
    router_part = jnp.einsum(
        "spe,spd->ed", logit_grad, expert_input, preferred_element_type=jnp.float32
    )
    expert_delta = jnp.einsum(
        "spe,de->spd", logit_grad, router_weight, preferred_element_type=jnp.float32
    )
    grad_rows = returned_grads.reshape(expert_num, seq_count, capacity, model_width).transpose(
        1, 0, 2, 3
    ).reshape(seq_count, expert_num * capacity, model_width)
    expert_delta = expert_delta + jnp.einsum(
        "smp,smd->spd",
        slot_table.reshape(seq_count, expert_num * capacity, pos_count),
        grad_rows,
        preferred_element_type=jnp.float32,
    )
    state_part, second_part = second_back(expert_delta)
    state_grad = state_part + upstream
    state_low = state_grad.astype(jnp.bfloat16)
    mixed_flat = jnp.einsum(
        "spe,de->spd", state_low, merge_weight, preferred_element_type=jnp.float32
    ).astype(jnp.bfloat16)
    mixed_grad = mixed_flat.reshape(seq_count, pos_count, heads_num, head_dimension)
    dot_rows = jnp.sum(mixed_grad.astype(jnp.float32) * attended, axis=-1)
    grad_packed = jnp.concatenate([mixed_flat, *split_parts(dot_rows, 3), stat_zeros], axis=-1)
    grad_whole = lax.all_gather(grad_packed, ("ctx", "dp"), axis=1, tiled=True)

    def columns_of(value):
        cut = value.reshape(seq_count, pos_count, owners, column_count).transpose(2, 0, 1, 3)
        return lax.all_to_all(cut, "expert", split_axis=0, concat_axis=0, tiled=True).reshape(
            owners * seq_count, pos_count, column_count
        )

    prob_grad = jnp.einsum(
        "sqhd,skhd->shqk", mixed_grad, value_heads, preferred_element_type=jnp.float32
    )
    row_dot = dot_rows.transpose(0, 2, 1)[..., None]
    score_grad = (prob_mass * (prob_grad - row_dot)).astype(jnp.bfloat16)
    query_back = (
        (
            jnp.einsum("shqk,skhd->sqhd", score_grad, key_heads, preferred_element_type=jnp.float32)
            * score_scale
        )
        .astype(jnp.bfloat16)
        .reshape(seq_count, pos_count, model_width)
    )
    bias_portion = jnp.einsum(
        "stey,aey->at",
        score_grad,
        bucket_table(distance, bucket_num).astype(jnp.bfloat16),
        preferred_element_type=jnp.float32,
    )
    own_keys = keys_local.reshape(seq_count, pos_count, heads_num, head_dimension)
    own_values = values_local.reshape(seq_count, pos_count, heads_num, head_dimension)

    def unpack(packed):
        main = packed[..., :model_width].reshape(seq_count, seq_len, heads_num, head_dimension)
        stat = packed[..., model_width:].astype(jnp.float32)
        joined = (
            stat[..., :heads_num]
            + stat[..., heads_num : 2 * heads_num]
            + stat[..., 2 * heads_num : 3 * heads_num]
        )
        return main, joined.transpose(0, 2, 1)[..., None]

    query_part_heads, total_piece = unpack(query_whole)
    grad_part_heads, dot_piece = unpack(grad_whole)
    gap = lax.iota(jnp.int32, seq_len)[:, None] - query_pos[None, :]
    seen = gap >= 0
    piece_bias = bias_grid(relative_bucket_bias, jnp.clip(gap, 0, seq_len - 1))
    raw_piece = (
        jnp.einsum(
            "sqhd,skhd->shqk", query_part_heads, own_keys, preferred_element_type=jnp.float32
        )
        * score_scale
        + piece_bias[None]
    )
    prob_piece = jnp.exp(jnp.where(seen[None, None], raw_piece, -1e30) - total_piece)
    grad_prob = jnp.einsum(
        "sqhd,skhd->shqk", grad_part_heads, own_values, preferred_element_type=jnp.float32
    )
    score_piece = (prob_piece * (grad_prob - dot_piece)).astype(jnp.bfloat16)
    key_back = (
        (
            jnp.einsum(
                "shqk,sqhd->skhd", score_piece, query_part_heads, preferred_element_type=jnp.float32
            )
            * score_scale
        )
        .astype(jnp.bfloat16)
        .reshape(seq_count, pos_count, model_width)
    )
    value_back = (
        jnp.einsum(
            "shqk,sqhd->skhd",
            prob_piece.astype(jnp.bfloat16),
            grad_part_heads,
            preferred_element_type=jnp.float32,
        )
        .astype(jnp.bfloat16)
        .reshape(seq_count, pos_count, model_width)
    )
    merge_part = jnp.einsum(
        "spd,spc->dc", mixed_all, columns_of(state_low), preferred_element_type=jnp.float32
    ).astype(jnp.bfloat16)
    merge_sum = lax.psum_scatter(
        merge_part, ("ctx", "dp"), scatter_dimension=0, tiled=True
    ).astype(jnp.float32)
    back_cut = jnp.stack(
        [
            part.reshape(seq_count, pos_count, owners, column_count).transpose(2, 0, 1, 3)
            for part in (query_back, key_back, value_back)
        ],
        axis=1,
    )
    back_all = lax.all_to_all(back_cut, "expert", split_axis=0, concat_axis=0, tiled=True)
    back_part = (
        jnp.einsum(
            "ospd,onspc->dnc",
            mixer_all.reshape(owners, seq_count, pos_count, model_width),
            back_all,
            preferred_element_type=jnp.float32,
        )
        .reshape(model_width, 3 * column_count)
        .astype(jnp.bfloat16)
    )
    back_sum = lax.psum_scatter(
        back_part, ("ctx", "dp"), scatter_dimension=0, tiled=True
    ).astype(jnp.float32)
    mixer_delta = jnp.einsum(
        "spe,de->spd", query_back, query_weight, preferred_element_type=jnp.float32
    )
    mixer_delta = mixer_delta + jnp.einsum(
        "spe,de->spd", key_back, key_weight, preferred_element_type=jnp.float32
    )
    mixer_delta = mixer_delta + jnp.einsum(
        "spe,de->spd", value_back, value_weight, preferred_element_type=jnp.float32
    )
    input_part, first_part = first_back(mixer_delta)
    input_grad = state_grad + input_part
    second_sum, router_sum = total_over((second_part, router_part), everyone)
    first_sum, bias_total = total_over((first_part, bias_portion), everyone)
    return (
        layer_output,
        input_grad,
        first_sum,
        back_sum[:, :column_count],
        back_sum[:, column_count : 2 * column_count],
        back_sum[:, 2 * column_count :],
        merge_sum,
        bias_total,
        second_sum,
        router_sum.T,
        gate_grad,
        up_grad,
        down_grad,
    )


def solution(mesh):
    in_specs = (
        P("expert", ("ctx", "dp"), None),
        P("expert", ("ctx", "dp"), None),
        P("expert", ("ctx", "dp"), None),
        P(),
        P(),
        P(),
        P(),
        P(),
        P(),
        P(),
        P(),
        P("expert", None, "ctx"),
        P("expert", None, "ctx"),
        P("expert", "ctx", None),
    )
    out_specs = (
        P("expert", ("ctx", "dp"), None),
        P("expert", ("ctx", "dp"), None),
        P(),
        P(("ctx", "dp"), "expert"),
        P(("ctx", "dp"), "expert"),
        P(("ctx", "dp"), "expert"),
        P(("ctx", "dp"), "expert"),
        P(),
        P(),
        P(),
        P("expert", "dp", "ctx"),
        P("expert", "dp", "ctx"),
        P("expert", "ctx", "dp"),
    )
    return jax.shard_map(
        per_device, mesh=mesh, in_specs=in_specs, out_specs=out_specs, check_vma=False
    )
```

```python
import math

import jax
import jax.numpy as jnp
from jax import lax
from jax.experimental import pallas as pl
from jax.experimental.pallas import tpu as pltpu
from jax.sharding import PartitionSpec as P

norm_eps = 1e-06
reach_span = 128.0


def bucket_bounds(bucket_num):
    exact_span = bucket_num // 2
    bounds = list(range(1, exact_span))
    for target in range(exact_span, bucket_num):
        border = exact_span
        while (
            exact_span
            + int(math.log(border / exact_span) / math.log(reach_span / exact_span) * exact_span)
            < target
        ):
            border += 1
        bounds.append(border)
    return bounds


def distance_buckets(distance, bucket_num):
    counted = jnp.zeros(distance.shape, jnp.int32)
    for border in bucket_bounds(bucket_num):
        counted = counted + (distance >= border).astype(jnp.int32)
    return counted


def rms_scale(values, gain_vec):
    return (
        values * lax.rsqrt(jnp.mean(values * values, axis=-1, keepdims=True) + norm_eps) * gain_vec
    )


def gated_hidden(gate_pre, up_pre):
    return jax.nn.gelu(gate_pre, approximate=False) * up_pre


def pair_softmax(logit_pair):
    return jax.nn.softmax(logit_pair, axis=-1)


def bucket_table(distance, bucket_num):
    bucket_of = distance_buckets(distance, bucket_num)
    return (lax.iota(jnp.int32, bucket_num)[:, None, None] == bucket_of[None]).astype(jnp.float32)


def split_parts(values, count):
    parts = []
    rest = values
    for _ in range(count):
        part = rest.astype(jnp.bfloat16)
        parts.append(part)
        rest = rest - part.astype(jnp.float32)
    return parts


def bias_grid(bias_table, distance):
    return jnp.einsum(
        "ry,rta->yta",
        bias_table,
        bucket_table(distance, bias_table.shape[0]),
        precision=lax.Precision.HIGHEST,
    )


def slot_hot(hits, capacity):
    pos_count = hits.shape[-1]
    before = (
        lax.iota(jnp.int32, pos_count)[:, None] < lax.iota(jnp.int32, pos_count)[None, :]
    ).astype(jnp.bfloat16)
    slots = jnp.einsum(
        "...p,pq->...q", hits.astype(jnp.bfloat16), before, preferred_element_type=jnp.float32
    ).astype(jnp.int32)
    rows = lax.iota(jnp.int32, capacity)[:, None]
    return jnp.where(
        hits[..., None, :] & (slots[..., None, :] == rows), 1.0, 0.0
    ).astype(jnp.bfloat16)


def flat_place(axes):
    place = 0
    for axis in axes:
        place = place * lax.axis_size(axis) + lax.axis_index(axis)
    return place


def device_at(axes, place):
    coordinates = {}
    for axis in reversed(axes):
        size = lax.axis_size(axis)
        coordinates[axis] = lax.rem(place, size)
        place = place // size
    return coordinates


def greet(axes, peers):
    barrier = pltpu.get_barrier_semaphore()
    for peer in peers:
        pl.semaphore_signal(
            barrier, inc=1, device_id=device_at(axes, peer), device_id_type=pl.DeviceIdType.MESH
        )
    pl.semaphore_wait(barrier, len(peers))


def exchange(arrays, axes, collective_id):
    count = lax.axis_size(axes)
    num = len(arrays)

    def kernel(*refs):
        sources, targets = refs[:num], refs[num : 2 * num]
        own_sem, send_sem, recv_sem = refs[2 * num :]
        me = flat_place(axes)
        peers = [lax.rem(me + step, count) for step in range(1, count)]
        owns = []
        for k in range(num):
            own = pltpu.make_async_copy(sources[k].at[me], targets[k].at[0], own_sem.at[k])
            own.start()
            owns.append(own)
        greet(axes, peers)
        copies = []
        for step, peer in enumerate(peers):
            for k in range(num):
                copy = pltpu.make_async_remote_copy(
                    src_ref=sources[k].at[peer],
                    dst_ref=targets[k].at[step + 1],
                    send_sem=send_sem.at[k, step],
                    recv_sem=recv_sem.at[k, step],
                    device_id=device_at(axes, peer),
                    device_id_type=pl.DeviceIdType.MESH,
                )
                copy.start()
                copies.append(copy)
        for copy in copies + owns:
            copy.wait()

    return pl.pallas_call(
        kernel,
        out_shape=[jax.ShapeDtypeStruct(array.shape, array.dtype) for array in arrays],
        in_specs=[pl.BlockSpec(memory_space=pl.ANY)] * num,
        out_specs=[pl.BlockSpec(memory_space=pl.ANY)] * num,
        scratch_shapes=[
            pltpu.SemaphoreType.DMA((num,)),
            pltpu.SemaphoreType.DMA((num, count - 1)),
            pltpu.SemaphoreType.DMA((num, count - 1)),
        ],
        compiler_params=pltpu.CompilerParams(collective_id=collective_id, has_side_effects=True),
    )(*arrays)


def flip(place, bit):
    return place + bit - 2 * bit * lax.rem(place // bit, 2)


def doubling_gather(arrays, axes, orders, collective_id):
    count = lax.axis_size(axes)
    num = len(arrays)
    stages = len(orders[0])

    def kernel(*refs):
        sources, targets = refs[:num], refs[num : 2 * num]
        own_sem, send_sem, recv_sem = refs[2 * num :]
        me = flat_place(axes)
        owns = []
        for k in range(num):
            own = pltpu.make_async_copy(sources[k], targets[k].at[me], own_sem.at[k])
            own.start()
            owns.append(own)
        greet(axes, [flip(me, 2**bit) for bit in range(stages)])
        held = [[me] for _ in range(num)]
        for stage in range(stages):
            copies = []
            for k in range(num):
                bit = 2 ** orders[k][stage]
                partner = device_at(axes, flip(me, bit))
                for slot, block in enumerate(held[k]):
                    lane = 2**stage - 1 + slot
                    copy = pltpu.make_async_remote_copy(
                        src_ref=sources[k] if stage == 0 else targets[k].at[block],
                        dst_ref=targets[k].at[block],
                        send_sem=send_sem.at[k, lane],
                        recv_sem=recv_sem.at[k, lane],
                        device_id=partner,
                        device_id_type=pl.DeviceIdType.MESH,
                    )
                    copy.start()
                    copies.append(copy)
                held[k] = held[k] + [flip(block, bit) for block in held[k]]
            if stage == 0:
                for own in owns:
                    own.wait()
            for copy in copies:
                copy.wait()

    return pl.pallas_call(
        kernel,
        out_shape=[jax.ShapeDtypeStruct((count, *array.shape), array.dtype) for array in arrays],
        in_specs=[pl.BlockSpec(memory_space=pl.ANY)] * num,
        out_specs=[pl.BlockSpec(memory_space=pl.ANY)] * num,
        scratch_shapes=[
            pltpu.SemaphoreType.DMA((num,)),
            pltpu.SemaphoreType.DMA((num, count - 1)),
            pltpu.SemaphoreType.DMA((num, count - 1)),
        ],
        compiler_params=pltpu.CompilerParams(collective_id=collective_id, has_side_effects=True),
    )(*arrays)


def doubling_orders():
    dp_bits = lax.axis_size("dp").bit_length() - 1
    ctx_bits = lax.axis_size("ctx").bit_length() - 1
    inner = list(range(dp_bits))
    outer = list(range(dp_bits + 1, dp_bits + ctx_bits))
    last = [dp_bits] if ctx_bits else []
    return inner + outer + last, outer + inner + last


def sum_everywhere(packed, phases, collective_id):
    counts = [lax.axis_size(axes) for axes in phases]
    rows, lanes = packed.shape

    def kernel(x_ref, out_ref, *scratch):
        barrier = pltpu.get_barrier_semaphore()
        peers = []
        for axes, count in zip(phases, counts):
            me = flat_place(axes)
            peers.append([lax.rem(me + step, count) for step in range(1, count)])
        for axes, group in zip(phases, peers):
            for peer in group:
                pl.semaphore_signal(
                    barrier,
                    inc=1,
                    device_id=device_at(axes, peer),
                    device_id_type=pl.DeviceIdType.MESH,
                )
        pl.semaphore_wait(barrier, sum(len(group) for group in peers))
        out_ref[...] = x_ref[...]
        for phase, axes in enumerate(phases):
            mine, landed, send_sem, recv_sem = scratch[4 * phase : 4 * phase + 4]
            mine[...] = out_ref[...]
            copies = []
            for step, peer in enumerate(peers[phase]):
                copy = pltpu.make_async_remote_copy(
                    src_ref=mine,
                    dst_ref=landed.at[step],
                    send_sem=send_sem.at[step],
                    recv_sem=recv_sem.at[step],
                    device_id=device_at(axes, peer),
                    device_id_type=pl.DeviceIdType.MESH,
                )
                copy.start()
                copies.append(copy)
            for step, copy in enumerate(copies):
                copy.wait()
                out_ref[...] += landed[step]

    scratch = []
    for count in counts:
        scratch += [
            pltpu.VMEM((rows, lanes), jnp.float32),
            pltpu.VMEM((count - 1, rows, lanes), jnp.float32),
            pltpu.SemaphoreType.DMA((count - 1,)),
            pltpu.SemaphoreType.DMA((count - 1,)),
        ]
    return pl.pallas_call(
        kernel,
        out_shape=jax.ShapeDtypeStruct(packed.shape, packed.dtype),
        in_specs=[pl.BlockSpec(memory_space=pltpu.VMEM)],
        out_specs=pl.BlockSpec(memory_space=pltpu.VMEM),
        scratch_shapes=scratch,
        compiler_params=pltpu.CompilerParams(collective_id=collective_id, has_side_effects=True),
    )(packed)


def total_over(values, collective_id):
    flat = jnp.concatenate([value.reshape(-1) for value in values])
    size = flat.shape[0]
    packed = jnp.pad(flat, (0, (-size) % 1024)).reshape(-1, 128)
    summed = sum_everywhere(packed, (("ctx", "dp"), ("expert",)), collective_id).reshape(-1)
    outs = []
    offset = 0
    for value in values:
        outs.append(summed[offset : offset + value.size].reshape(value.shape))
        offset += value.size
    return outs


def shifted(value, axis, step):
    size = lax.axis_size(axis)
    return lax.ppermute(value, axis, [(i, (i + step) % size) for i in range(size)])


def gather_back(value, axis):
    size = lax.axis_size(axis)
    return jnp.stack([value] + [shifted(value, axis, step) for step in range(1, size)])


def exchange_back(blocks, axis):
    size = lax.axis_size(axis)
    me = lax.axis_index(axis)
    parts = [lax.dynamic_index_in_dim(blocks, me, 0, keepdims=False)]
    for step in range(1, size):
        block = lax.dynamic_index_in_dim(blocks, lax.rem(me + step, size), 0, keepdims=False)
        parts.append(shifted(block, axis, step))
    return jnp.stack(parts)


def from_places(stacked, axis):
    size = lax.axis_size(axis)
    order = lax.rem(lax.axis_index(axis) - lax.iota(jnp.int32, size) + size, size)
    return jnp.take(stacked, order, axis=0)


def per_device(
    inputs,
    cotangent,
    expert_ids,
    first_gain,
    query_weight,
    key_weight,
    value_weight,
    merge_weight,
    relative_bucket_bias,
    expert_norm_gain,
    router_weight,
    gate_weight,
    up_weight,
    down_weight,
):
    seq_count, pos_count, model_width = inputs.shape
    bucket_num, heads_num = relative_bucket_bias.shape
    head_dimension = model_width // heads_num
    score_scale = head_dimension ** (-0.5)
    expert_num = router_weight.shape[1]
    local_experts = gate_weight.shape[0]
    owners = lax.axis_size("expert")
    places = lax.axis_size(("ctx", "dp"))
    seq_len = pos_count * places
    capacity = min(pos_count, max(2, 9 * pos_count // (4 * expert_num)))
    lane_rows = seq_count * capacity
    line_order, other_order = doubling_orders()
    row_order = [bit for bit in range(1, lax.axis_size("ctx").bit_length() - 1)] + [0]
    column_count = model_width // owners
    first_expert = lax.axis_index("expert") * local_experts
    id_zeros = jnp.zeros((seq_count, pos_count, 126), jnp.bfloat16)
    cotangent_all = lax.all_gather(
        jnp.concatenate([cotangent, expert_ids.astype(jnp.bfloat16), id_zeros], axis=-1),
        ("ctx", "expert"),
        axis=0,
        tiled=True,
    )
    ids_all = cotangent_all[..., model_width : model_width + 2].astype(jnp.int32)
    block_num = ids_all.shape[0]
    residual = inputs.astype(jnp.float32)
    first_normed, first_back = jax.vjp(rms_scale, residual, first_gain)
    mixer_in = first_normed.astype(jnp.bfloat16)
    keys_local = jnp.einsum(
        "spd,de->spe", mixer_in, key_weight, preferred_element_type=jnp.float32
    ).astype(jnp.bfloat16)
    values_local = jnp.einsum(
        "spd,de->spe", mixer_in, value_weight, preferred_element_type=jnp.float32
    ).astype(jnp.bfloat16)
    keys_whole, values_whole = (
        whole.transpose(1, 0, 2, 3).reshape(seq_count, seq_len, model_width)
        for whole in doubling_gather(
            (keys_local, values_local), ("ctx", "dp"), (line_order, other_order), 1
        )
    )
    queries = jnp.einsum(
        "spd,de->spe", mixer_in, query_weight, preferred_element_type=jnp.float32
    ).astype(jnp.bfloat16)
    query_heads = queries.reshape(seq_count, pos_count, heads_num, head_dimension)
    key_heads = keys_whole.reshape(seq_count, seq_len, heads_num, head_dimension)
    value_heads = values_whole.reshape(seq_count, seq_len, heads_num, head_dimension)
    first_pos = lax.axis_index(("ctx", "dp")) * pos_count
    query_pos = first_pos + lax.iota(jnp.int32, pos_count)
    offsets = query_pos[:, None] - lax.iota(jnp.int32, seq_len)[None, :]
    visible = offsets >= 0
    distance = jnp.clip(offsets, 0, seq_len - 1)
    bias_lattice = bias_grid(relative_bucket_bias, distance)
    raw_scores = (
        jnp.einsum("sqhd,skhd->shqk", query_heads, key_heads, preferred_element_type=jnp.float32)
        * score_scale
        + bias_lattice[None]
    )
    masked = jnp.where(visible[None, None], raw_scores, -1e30)
    row_top = jnp.max(masked, axis=-1, keepdims=True)
    exp_terms = jnp.exp(masked - row_top)
    row_total = jnp.sum(exp_terms, axis=-1, keepdims=True)
    prob_mass = exp_terms / row_total
    log_total = row_top + jnp.log(row_total)
    attended = jnp.einsum(
        "shqk,skhd->sqhd",
        prob_mass.astype(jnp.bfloat16),
        value_heads,
        preferred_element_type=jnp.float32,
    )
    total_rows = log_total[..., 0].transpose(0, 2, 1)
    stat_pad = -(-3 * heads_num // 128) * 128 - 3 * heads_num
    stat_zeros = jnp.zeros((seq_count, pos_count, stat_pad), jnp.bfloat16)
    query_packed = jnp.concatenate([queries, *split_parts(total_rows, 3), stat_zeros], axis=-1)
    mixer_all = gather_back(mixer_in, "expert")
    mixed_heads = attended.reshape(seq_count, pos_count, model_width).astype(jnp.bfloat16)
    hidden_state = residual + jnp.einsum(
        "spd,de->spe", mixed_heads, merge_weight, preferred_element_type=jnp.float32
    )
    second_normed, second_back = jax.vjp(rms_scale, hidden_state, expert_norm_gain)
    expert_input = second_normed.astype(jnp.bfloat16)
    own_hits = jnp.any(
        expert_ids[None] == lax.iota(jnp.int32, expert_num)[:, None, None, None], axis=-1
    )
    own_hot = slot_hot(own_hits, capacity)
    dispatched = (
        jnp.einsum("eskp,spd->eskd", own_hot, expert_input, preferred_element_type=jnp.float32)
        .astype(jnp.bfloat16)
        .reshape(owners, local_experts, lane_rows, model_width)
    )
    arrived = from_places(exchange((dispatched,), ("expert",), 2)[0], "expert")
    slot_rows = arrived.transpose(1, 0, 2, 3).reshape(
        local_experts, owners * lane_rows, model_width
    )
    (rows_whole,) = doubling_gather((slot_rows,), ("ctx",), (row_order,), 3)
    all_rows = rows_whole.transpose(1, 0, 2, 3).reshape(
        local_experts, block_num * capacity, model_width
    )
    my_experts = first_expert + lax.iota(jnp.int32, local_experts)
    block_hits = jnp.any(ids_all[None] == my_experts[:, None, None, None], axis=-1)
    block_hot = slot_hot(block_hits, capacity)
    other_ids = jnp.sum(ids_all, axis=-1)[None] - my_experts[:, None, None]
    row_other = jnp.sum(
        block_hot.astype(jnp.float32) * other_ids[:, :, None, :].astype(jnp.float32), axis=-1
    ).astype(jnp.int32).reshape(local_experts, block_num * capacity)
    cotangent_rows = jnp.einsum(
        "lbkp,bpd->lbkd", block_hot, cotangent_all[..., :model_width], preferred_element_type=jnp.float32
    ).astype(jnp.bfloat16).reshape(local_experts, block_num * capacity, model_width)
    row_logits = jnp.einsum(
        "lrd,de->lre", all_rows, router_weight, preferred_element_type=jnp.float32
    )
    expert_line = lax.iota(jnp.int32, expert_num)[None, None, :]
    own_logit = jnp.sum(
        jnp.where(expert_line == my_experts[:, None, None], row_logits, 0.0), axis=-1
    )
    other_logit = jnp.sum(jnp.where(expert_line == row_other[..., None], row_logits, 0.0), axis=-1)
    row_gates = jax.nn.sigmoid(own_logit - other_logit)
    all_grads = (row_gates[..., None] * cotangent_rows.astype(jnp.float32)).astype(jnp.bfloat16)
    gate_pre = jnp.einsum("erd,edf->erf", all_rows, gate_weight, preferred_element_type=jnp.float32)
    up_pre = jnp.einsum("erd,edf->erf", all_rows, up_weight, preferred_element_type=jnp.float32)
    hidden_float, act_back = jax.vjp(gated_hidden, gate_pre, up_pre)
    hidden_act = hidden_float.astype(jnp.bfloat16)
    partial_value = jnp.einsum(
        "erf,efd->erd", hidden_act, down_weight, preferred_element_type=jnp.float32
    ).astype(jnp.bfloat16)
    partial_value, all_grads = lax.optimization_barrier((partial_value, all_grads))
    expert_result = lax.psum_scatter(partial_value, "ctx", scatter_dimension=1, tiled=True)
    returning = expert_result.reshape(local_experts, owners, lane_rows, model_width).transpose(
        1, 0, 2, 3
    )
    hidden_grad = jnp.einsum(
        "erd,efd->erf", all_grads, down_weight, preferred_element_type=jnp.float32
    )
    gate_delta, up_delta = act_back(hidden_grad)
    gate_low = gate_delta.astype(jnp.bfloat16)
    up_low = up_delta.astype(jnp.bfloat16)
    row_part = (
        jnp.einsum("erf,edf->erd", gate_low, gate_weight, preferred_element_type=jnp.float32)
        + jnp.einsum("erf,edf->erd", up_low, up_weight, preferred_element_type=jnp.float32)
    ).astype(jnp.bfloat16)
    row_blocks = row_part.reshape(local_experts, -1, owners * lane_rows, model_width)
    (row_landed,) = exchange((row_blocks.transpose(1, 0, 2, 3),), ("ctx",), 4)
    row_grads = jnp.sum(row_landed.astype(jnp.float32), axis=0).astype(jnp.bfloat16)
    back_rows = row_grads.reshape(local_experts, owners, lane_rows, model_width).transpose(
        1, 0, 2, 3
    )
    returned, returned_grads = (
        from_places(landed, "expert")
        for landed in exchange((returning, back_rows), ("expert",), 5)
    )
    mixed_all = gather_back(mixed_heads, "expert")
    query_whole = lax.all_gather(query_packed, ("ctx", "dp"), axis=1, tiled=True)
    down_part = jnp.einsum(
        "erf,erd->efd", hidden_act, all_grads, preferred_element_type=jnp.float32
    )
    gate_part = jnp.einsum("erd,erf->edf", all_rows, gate_low, preferred_element_type=jnp.float32)
    up_part = jnp.einsum("erd,erf->edf", all_rows, up_low, preferred_element_type=jnp.float32)
    gate_grad, up_grad, down_grad = (
        lax.psum_scatter(
            gate_part.astype(jnp.bfloat16), "dp", scatter_dimension=1, tiled=True
        ).astype(jnp.float32),
        lax.psum_scatter(
            up_part.astype(jnp.bfloat16), "dp", scatter_dimension=1, tiled=True
        ).astype(jnp.float32),
        lax.psum_scatter(
            down_part.astype(jnp.bfloat16), "dp", scatter_dimension=2, tiled=True
        ).astype(jnp.float32),
    )
    logits = jnp.einsum(
        "spd,de->spe", expert_input, router_weight, preferred_element_type=jnp.float32
    )
    pick_hot = expert_ids[..., None] == lax.iota(jnp.int32, expert_num)
    picked_logits = jnp.sum(jnp.where(pick_hot, logits[:, :, None, :], 0.0), axis=-1)
    gate_values, gate_back = jax.vjp(pair_softmax, picked_logits)
    upstream = cotangent.astype(jnp.float32)
    slot_table = own_hot.transpose(1, 0, 2, 3)
    choose = (
        slot_table[:, None] * pick_hot.transpose(0, 2, 3, 1)[:, :, :, None, :].astype(jnp.bfloat16)
    ).reshape(seq_count, 2, expert_num * capacity, pos_count)
    returned_rows = returned.reshape(expert_num, seq_count, capacity, model_width).transpose(
        1, 0, 2, 3
    ).reshape(seq_count, expert_num * capacity, model_width)
    picked = jnp.einsum(
        "sjmp,smd->sjpd", choose, returned_rows, preferred_element_type=jnp.float32
    )
    expert_sum = (
        gate_values[:, :, 0, None] * picked[:, 0] + gate_values[:, :, 1, None] * picked[:, 1]
    )
    layer_output = (hidden_state + expert_sum).astype(jnp.bfloat16)
    pair_delta = jnp.sum(upstream[:, None] * picked, axis=-1).transpose(0, 2, 1)
    (pick_grad,) = gate_back(pair_delta)
    logit_grad = jnp.sum(jnp.where(pick_hot, pick_grad[..., None], 0.0), axis=2).astype(
        jnp.bfloat16
    )
    router_part = jnp.einsum(
        "spe,spd->ed", logit_grad, expert_input, preferred_element_type=jnp.float32
    )
    expert_delta = jnp.einsum(
        "spe,de->spd", logit_grad, router_weight, preferred_element_type=jnp.float32
    )
    grad_rows = returned_grads.reshape(expert_num, seq_count, capacity, model_width).transpose(
        1, 0, 2, 3
    ).reshape(seq_count, expert_num * capacity, model_width)
    expert_delta = expert_delta + jnp.einsum(
        "smp,smd->spd",
        slot_table.reshape(seq_count, expert_num * capacity, pos_count),
        grad_rows,
        preferred_element_type=jnp.float32,
    )
    state_part, second_part = second_back(expert_delta)
    state_grad = state_part + upstream
    state_low = state_grad.astype(jnp.bfloat16)
    mixed_flat = jnp.einsum(
        "spe,de->spd", state_low, merge_weight, preferred_element_type=jnp.float32
    ).astype(jnp.bfloat16)
    mixed_grad = mixed_flat.reshape(seq_count, pos_count, heads_num, head_dimension)
    prob_grad = jnp.einsum(
        "sqhd,skhd->shqk", mixed_grad, value_heads, preferred_element_type=jnp.float32
    )
    row_dot = jnp.sum(prob_mass * prob_grad, axis=-1, keepdims=True)
    dot_rows = row_dot[..., 0].transpose(0, 2, 1)
    grad_packed = jnp.concatenate([mixed_flat, *split_parts(dot_rows, 3), stat_zeros], axis=-1)
    grad_whole = jnp.concatenate(
        [
            whole.transpose(1, 0, 2, 3).reshape(seq_count, seq_len, -1)
            for whole in doubling_gather(
                (grad_packed[..., : model_width // 2], grad_packed[..., model_width // 2 :]),
                ("ctx", "dp"),
                (line_order, other_order),
                6,
            )
        ],
        axis=-1,
    )

    def columns_of(value):
        return value.reshape(seq_count, pos_count, owners, column_count).transpose(2, 0, 1, 3)

    score_grad = (prob_mass * (prob_grad - row_dot)).astype(jnp.bfloat16)
    query_back = (
        (
            jnp.einsum("shqk,skhd->sqhd", score_grad, key_heads, preferred_element_type=jnp.float32)
            * score_scale
        )
        .astype(jnp.bfloat16)
        .reshape(seq_count, pos_count, model_width)
    )
    bias_portion = jnp.einsum(
        "stey,aey->at",
        score_grad,
        bucket_table(distance, bucket_num).astype(jnp.bfloat16),
        preferred_element_type=jnp.float32,
    )
    own_keys = keys_local.reshape(seq_count, pos_count, heads_num, head_dimension)
    own_values = values_local.reshape(seq_count, pos_count, heads_num, head_dimension)

    def unpack(packed):
        main = packed[..., :model_width].reshape(seq_count, seq_len, heads_num, head_dimension)
        stat = packed[..., model_width:].astype(jnp.float32)
        joined = (
            stat[..., :heads_num]
            + stat[..., heads_num : 2 * heads_num]
            + stat[..., 2 * heads_num : 3 * heads_num]
        )
        return main, joined.transpose(0, 2, 1)[..., None]

    query_part_heads, total_piece = unpack(query_whole)
    grad_part_heads, dot_piece = unpack(grad_whole)
    gap = lax.iota(jnp.int32, seq_len)[:, None] - query_pos[None, :]
    seen = gap >= 0
    piece_bias = bias_grid(relative_bucket_bias, jnp.clip(gap, 0, seq_len - 1))
    raw_piece = (
        jnp.einsum(
            "sqhd,skhd->shqk", query_part_heads, own_keys, preferred_element_type=jnp.float32
        )
        * score_scale
        + piece_bias[None]
    )
    prob_piece = jnp.exp(jnp.where(seen[None, None], raw_piece, -1e30) - total_piece)
    grad_prob = jnp.einsum(
        "sqhd,skhd->shqk", grad_part_heads, own_values, preferred_element_type=jnp.float32
    )
    score_piece = (prob_piece * (grad_prob - dot_piece)).astype(jnp.bfloat16)
    key_back = (
        (
            jnp.einsum(
                "shqk,sqhd->skhd", score_piece, query_part_heads, preferred_element_type=jnp.float32
            )
            * score_scale
        )
        .astype(jnp.bfloat16)
        .reshape(seq_count, pos_count, model_width)
    )
    value_back = (
        jnp.einsum(
            "shqk,sqhd->skhd",
            prob_piece.astype(jnp.bfloat16),
            grad_part_heads,
            preferred_element_type=jnp.float32,
        )
        .astype(jnp.bfloat16)
        .reshape(seq_count, pos_count, model_width)
    )
    merge_part = jnp.einsum(
        "ospd,ospc->dc",
        mixed_all,
        exchange_back(columns_of(state_low), "expert"),
        preferred_element_type=jnp.float32,
    )
    back_cut = jnp.stack(
        [columns_of(part) for part in (query_back, key_back, value_back)], axis=1
    )
    (back_all,) = exchange((back_cut,), ("expert",), 7)
    back_part = jnp.einsum(
        "ospd,onspc->dnc", mixer_all, back_all, preferred_element_type=jnp.float32
    ).reshape(model_width, 3 * column_count)
    dense_part = jnp.concatenate([back_part, merge_part], axis=1).astype(jnp.bfloat16)
    (dense_landed,) = exchange(
        (dense_part.reshape(places, model_width // places, 4 * column_count),), ("ctx", "dp"), 8
    )
    back_sum = jnp.sum(dense_landed.astype(jnp.float32), axis=0)
    mixer_delta = jnp.einsum(
        "spe,de->spd", query_back, query_weight, preferred_element_type=jnp.float32
    )
    mixer_delta = mixer_delta + jnp.einsum(
        "spe,de->spd", key_back, key_weight, preferred_element_type=jnp.float32
    )
    mixer_delta = mixer_delta + jnp.einsum(
        "spe,de->spd", value_back, value_weight, preferred_element_type=jnp.float32
    )
    input_part, first_part = first_back(mixer_delta)
    input_grad = state_grad + input_part
    first_sum, second_sum, router_sum, bias_total = total_over(
        (first_part, second_part, router_part, bias_portion), 9
    )
    return (
        layer_output,
        input_grad,
        first_sum,
        back_sum[:, :column_count],
        back_sum[:, column_count : 2 * column_count],
        back_sum[:, 2 * column_count : 3 * column_count],
        back_sum[:, 3 * column_count :],
        bias_total,
        second_sum,
        router_sum.T,
        gate_grad,
        up_grad,
        down_grad,
    )


def solution(mesh):
    in_specs = (
        P("expert", ("ctx", "dp"), None),
        P("expert", ("ctx", "dp"), None),
        P("expert", ("ctx", "dp"), None),
        P(),
        P(),
        P(),
        P(),
        P(),
        P(),
        P(),
        P(),
        P("expert", None, "ctx"),
        P("expert", None, "ctx"),
        P("expert", "ctx", None),
    )
    out_specs = (
        P("expert", ("ctx", "dp"), None),
        P("expert", ("ctx", "dp"), None),
        P(),
        P(("ctx", "dp"), "expert"),
        P(("ctx", "dp"), "expert"),
        P(("ctx", "dp"), "expert"),
        P(("ctx", "dp"), "expert"),
        P(),
        P(),
        P(),
        P("expert", "dp", "ctx"),
        P("expert", "dp", "ctx"),
        P("expert", "ctx", "dp"),
    )
    return jax.shard_map(
        per_device, mesh=mesh, in_specs=in_specs, out_specs=out_specs, check_vma=False
    )
```

```python
import math

import jax
import jax.numpy as jnp
from jax import lax
from jax.experimental import pallas as pl
from jax.experimental.pallas import tpu as pltpu
from jax.sharding import PartitionSpec as P

norm_eps = 1e-06
reach_span = 128.0


def bucket_bounds(bucket_num):
    exact_span = bucket_num // 2
    bounds = list(range(1, exact_span))
    for target in range(exact_span, bucket_num):
        border = exact_span
        while (
            exact_span
            + int(math.log(border / exact_span) / math.log(reach_span / exact_span) * exact_span)
            < target
        ):
            border += 1
        bounds.append(border)
    return bounds


def distance_buckets(distance, bucket_num):
    counted = jnp.zeros(distance.shape, jnp.int32)
    for border in bucket_bounds(bucket_num):
        counted = counted + (distance >= border).astype(jnp.int32)
    return counted


def rms_scale(values, gain_vec):
    return (
        values * lax.rsqrt(jnp.mean(values * values, axis=-1, keepdims=True) + norm_eps) * gain_vec
    )


def gated_hidden(gate_pre, up_pre):
    return jax.nn.gelu(gate_pre, approximate=False) * up_pre


def pair_softmax(logit_pair):
    return jax.nn.softmax(logit_pair, axis=-1)


def bucket_table(distance, bucket_num):
    bucket_of = distance_buckets(distance, bucket_num)
    return (lax.iota(jnp.int32, bucket_num)[:, None, None] == bucket_of[None]).astype(jnp.float32)


def split_parts(values, count):
    parts = []
    rest = values
    for _ in range(count):
        part = rest.astype(jnp.bfloat16)
        parts.append(part)
        rest = rest - part.astype(jnp.float32)
    return parts


def bias_grid(bias_table, distance):
    return jnp.einsum(
        "ry,rta->yta",
        bias_table,
        bucket_table(distance, bias_table.shape[0]),
        precision=lax.Precision.HIGHEST,
    )


def slot_hot(hits, capacity):
    pos_count = hits.shape[-1]
    before = (
        lax.iota(jnp.int32, pos_count)[:, None] < lax.iota(jnp.int32, pos_count)[None, :]
    ).astype(jnp.bfloat16)
    slots = jnp.einsum(
        "...p,pq->...q", hits.astype(jnp.bfloat16), before, preferred_element_type=jnp.float32
    ).astype(jnp.int32)
    rows = lax.iota(jnp.int32, capacity)[:, None]
    return jnp.where(
        hits[..., None, :] & (slots[..., None, :] == rows), 1.0, 0.0
    ).astype(jnp.bfloat16)


def flat_place(axes):
    place = 0
    for axis in axes:
        place = place * lax.axis_size(axis) + lax.axis_index(axis)
    return place


def device_at(axes, place):
    coordinates = {}
    for axis in reversed(axes):
        size = lax.axis_size(axis)
        coordinates[axis] = lax.rem(place, size)
        place = place // size
    return coordinates


def greet(axes, peers):
    barrier = pltpu.get_barrier_semaphore()
    for peer in peers:
        pl.semaphore_signal(
            barrier, inc=1, device_id=device_at(axes, peer), device_id_type=pl.DeviceIdType.MESH
        )
    pl.semaphore_wait(barrier, len(peers))


def exchange(arrays, axes, collective_id, by_place=True):
    count = lax.axis_size(axes)
    num = len(arrays)

    def kernel(*refs):
        sources, targets = refs[:num], refs[num : 2 * num]
        own_sem, send_sem, recv_sem = refs[2 * num :]
        me = flat_place(axes)
        peers = [lax.rem(me + step, count) for step in range(1, count)]
        owns = []
        for k in range(num):
            own = pltpu.make_async_copy(sources[k].at[me], targets[k].at[me if by_place else 0], own_sem.at[k])
            own.start()
            owns.append(own)
        greet(axes, peers)
        copies = []
        for step, peer in enumerate(peers):
            for k in range(num):
                copy = pltpu.make_async_remote_copy(
                    src_ref=sources[k].at[peer],
                    dst_ref=targets[k].at[me if by_place else step + 1],
                    send_sem=send_sem.at[k, step],
                    recv_sem=recv_sem.at[k, step],
                    device_id=device_at(axes, peer),
                    device_id_type=pl.DeviceIdType.MESH,
                )
                copy.start()
                copies.append(copy)
        for copy in copies + owns:
            copy.wait()

    return pl.pallas_call(
        kernel,
        out_shape=[jax.ShapeDtypeStruct(array.shape, array.dtype) for array in arrays],
        in_specs=[pl.BlockSpec(memory_space=pl.ANY)] * num,
        out_specs=[pl.BlockSpec(memory_space=pl.ANY)] * num,
        scratch_shapes=[
            pltpu.SemaphoreType.DMA((num,)),
            pltpu.SemaphoreType.DMA((num, count - 1)),
            pltpu.SemaphoreType.DMA((num, count - 1)),
        ],
        compiler_params=pltpu.CompilerParams(collective_id=collective_id, has_side_effects=True),
    )(*arrays)


def flip(place, bit):
    return place + bit - 2 * bit * lax.rem(place // bit, 2)


def doubling_gather(arrays, axes, orders, collective_id):
    count = lax.axis_size(axes)
    num = len(arrays)
    stages = len(orders[0])
    pieces = []
    for k in range(num):
        rows = arrays[k].shape[1] // len(orders)
        pieces += [(k, n * rows, rows, order) for n, order in enumerate(orders)]

    def kernel(*refs):
        sources, targets = refs[:num], refs[num : 2 * num]
        own_sem, send_sem, recv_sem = refs[2 * num :]
        me = flat_place(axes)
        owns = []
        for k in range(num):
            own = pltpu.make_async_copy(sources[k], targets[k].at[me], own_sem.at[k])
            own.start()
            owns.append(own)
        greet(axes, [flip(me, 2**bit) for bit in range(stages)])
        held = [[me] for _ in pieces]
        for stage in range(stages):
            copies = []
            for p, (k, start, rows, order) in enumerate(pieces):
                bit = 2 ** order[stage]
                partner = device_at(axes, flip(me, bit))
                span = pl.ds(start, rows)
                for slot, block in enumerate(held[p]):
                    lane = 2**stage - 1 + slot
                    target = targets[k].at[block, :, span]
                    copy = pltpu.make_async_remote_copy(
                        src_ref=sources[k].at[:, span] if stage == 0 else target,
                        dst_ref=target,
                        send_sem=send_sem.at[p, lane],
                        recv_sem=recv_sem.at[p, lane],
                        device_id=partner,
                        device_id_type=pl.DeviceIdType.MESH,
                    )
                    copy.start()
                    copies.append(copy)
                held[p] = held[p] + [flip(block, bit) for block in held[p]]
            if stage == 0:
                for own in owns:
                    own.wait()
            for copy in copies:
                copy.wait()

    return pl.pallas_call(
        kernel,
        out_shape=[jax.ShapeDtypeStruct((count, *array.shape), array.dtype) for array in arrays],
        in_specs=[pl.BlockSpec(memory_space=pl.ANY)] * num,
        out_specs=[pl.BlockSpec(memory_space=pl.ANY)] * num,
        scratch_shapes=[
            pltpu.SemaphoreType.DMA((num,)),
            pltpu.SemaphoreType.DMA((len(pieces), count - 1)),
            pltpu.SemaphoreType.DMA((len(pieces), count - 1)),
        ],
        compiler_params=pltpu.CompilerParams(collective_id=collective_id, has_side_effects=True),
    )(*arrays)


def doubling_orders():
    dp_bits = lax.axis_size("dp").bit_length() - 1
    ctx_bits = lax.axis_size("ctx").bit_length() - 1
    inner = list(range(dp_bits))
    outer = list(range(dp_bits + 1, dp_bits + ctx_bits))
    last = [dp_bits] if ctx_bits else []
    return inner + outer + last, outer + inner + last


def sum_everywhere(packed, phases, collective_id):
    counts = [lax.axis_size(axes) for axes in phases]
    rows, lanes = packed.shape

    def kernel(x_ref, out_ref, *scratch):
        barrier = pltpu.get_barrier_semaphore()
        peers = []
        for axes, count in zip(phases, counts):
            me = flat_place(axes)
            peers.append([lax.rem(me + step, count) for step in range(1, count)])
        for axes, group in zip(phases, peers):
            for peer in group:
                pl.semaphore_signal(
                    barrier,
                    inc=1,
                    device_id=device_at(axes, peer),
                    device_id_type=pl.DeviceIdType.MESH,
                )
        pl.semaphore_wait(barrier, sum(len(group) for group in peers))
        out_ref[...] = x_ref[...]
        for phase, axes in enumerate(phases):
            mine, landed, send_sem, recv_sem = scratch[4 * phase : 4 * phase + 4]
            mine[...] = out_ref[...]
            copies = []
            for step, peer in enumerate(peers[phase]):
                copy = pltpu.make_async_remote_copy(
                    src_ref=mine,
                    dst_ref=landed.at[step],
                    send_sem=send_sem.at[step],
                    recv_sem=recv_sem.at[step],
                    device_id=device_at(axes, peer),
                    device_id_type=pl.DeviceIdType.MESH,
                )
                copy.start()
                copies.append(copy)
            for step, copy in enumerate(copies):
                copy.wait()
                out_ref[...] += landed[step]

    scratch = []
    for count in counts:
        scratch += [
            pltpu.VMEM((rows, lanes), jnp.float32),
            pltpu.VMEM((count - 1, rows, lanes), jnp.float32),
            pltpu.SemaphoreType.DMA((count - 1,)),
            pltpu.SemaphoreType.DMA((count - 1,)),
        ]
    return pl.pallas_call(
        kernel,
        out_shape=jax.ShapeDtypeStruct(packed.shape, packed.dtype),
        in_specs=[pl.BlockSpec(memory_space=pltpu.VMEM)],
        out_specs=pl.BlockSpec(memory_space=pltpu.VMEM),
        scratch_shapes=scratch,
        compiler_params=pltpu.CompilerParams(collective_id=collective_id, has_side_effects=True),
    )(packed)


def total_over(values, collective_id):
    flat = jnp.concatenate([value.reshape(-1) for value in values])
    size = flat.shape[0]
    packed = jnp.pad(flat, (0, (-size) % 1024)).reshape(-1, 128)
    summed = sum_everywhere(packed, (("ctx", "dp"), ("expert",)), collective_id).reshape(-1)
    outs = []
    offset = 0
    for value in values:
        outs.append(summed[offset : offset + value.size].reshape(value.shape))
        offset += value.size
    return outs


def shifted(value, axis, step):
    size = lax.axis_size(axis)
    return lax.ppermute(value, axis, [(i, (i + step) % size) for i in range(size)])


def gather_back(value, axis):
    size = lax.axis_size(axis)
    return jnp.stack([value] + [shifted(value, axis, step) for step in range(1, size)])


def exchange_back(blocks, axis):
    size = lax.axis_size(axis)
    me = lax.axis_index(axis)
    parts = [lax.dynamic_index_in_dim(blocks, me, 0, keepdims=False)]
    for step in range(1, size):
        block = lax.dynamic_index_in_dim(blocks, lax.rem(me + step, size), 0, keepdims=False)
        parts.append(shifted(block, axis, step))
    return jnp.stack(parts)


def lanes_dot(a, b):
    return lax.dot_general(a, b, (((1,), (1,)), ((), ())), preferred_element_type=jnp.float32)


def attend(queries, keys, values, bias, seen, width, scale):
    seq_count, pos_count, model_width = queries.shape
    seq_len = keys.shape[1]
    block = 128
    group = block // width
    groups = model_width // block

    def kernel(q_ref, k_ref, v_ref, bias_ref, seen_ref, mixed_ref, total_ref):
        for h in range(group):
            cut = slice(h * width, (h + 1) * width)
            scores = lanes_dot(q_ref[0, :, cut], k_ref[0, :, cut]) * scale + bias_ref[h]
            scores = jnp.where(seen_ref[...] > 0.0, scores, -1e30)
            top = jnp.max(scores, axis=-1, keepdims=True)
            terms = jnp.exp(scores - top)
            total = jnp.sum(terms, axis=-1, keepdims=True)
            attention = (terms / total).astype(jnp.bfloat16)
            mixed = jnp.dot(attention, v_ref[0, :, cut], preferred_element_type=jnp.float32)
            mixed_ref[0, :, cut] = mixed.astype(jnp.bfloat16)
            total_ref[0, 0, :, h : h + 1] = top + jnp.log(total)

    own = pl.BlockSpec((1, pos_count, block), lambda s, g: (s, 0, g))
    whole = pl.BlockSpec((1, seq_len, block), lambda s, g: (s, 0, g))
    return pl.pallas_call(
        kernel,
        grid=(seq_count, groups),
        in_specs=[
            own,
            whole,
            whole,
            pl.BlockSpec((group, pos_count, seq_len), lambda s, g: (g, 0, 0)),
            pl.BlockSpec((pos_count, seq_len), lambda s, g: (0, 0)),
        ],
        out_specs=[own, pl.BlockSpec((1, 1, pos_count, group), lambda s, g: (s, g, 0, 0))],
        out_shape=[
            jax.ShapeDtypeStruct(queries.shape, jnp.bfloat16),
            jax.ShapeDtypeStruct((seq_count, groups, pos_count, group), jnp.float32),
        ],
        compiler_params=pltpu.CompilerParams(vmem_limit_bytes=48 * 2**20),
    )(queries, keys, values, bias, seen)


def attend_back_queries(queries, keys, values, grads, bias, seen, totals, width, scale):
    seq_count, pos_count, model_width = queries.shape
    seq_len = keys.shape[1]
    block = 128
    group = block // width
    groups = model_width // block

    def kernel(
        q_ref, k_ref, v_ref, g_ref, bias_ref, seen_ref, total_ref, back_ref, dot_ref, score_ref
    ):
        for h in range(group):
            cut = slice(h * width, (h + 1) * width)
            scores = lanes_dot(q_ref[0, :, cut], k_ref[0, :, cut]) * scale + bias_ref[h]
            scores = jnp.where(seen_ref[...] > 0.0, scores, -1e30)
            attention = jnp.exp(scores - total_ref[0, 0, :, h : h + 1])
            prob_grad = lanes_dot(g_ref[0, :, cut], v_ref[0, :, cut])
            row_dot = jnp.sum(attention * prob_grad, axis=-1, keepdims=True)
            score_grad = (attention * (prob_grad - row_dot)).astype(jnp.bfloat16)
            back = jnp.dot(score_grad, k_ref[0, :, cut], preferred_element_type=jnp.float32)
            back_ref[0, :, cut] = (back * scale).astype(jnp.bfloat16)
            dot_ref[0, 0, :, h : h + 1] = row_dot
            score_ref[0, h] = score_grad

    own = pl.BlockSpec((1, pos_count, block), lambda s, g: (s, 0, g))
    whole = pl.BlockSpec((1, seq_len, block), lambda s, g: (s, 0, g))
    stat = pl.BlockSpec((1, 1, pos_count, group), lambda s, g: (s, g, 0, 0))
    return pl.pallas_call(
        kernel,
        grid=(seq_count, groups),
        in_specs=[
            own,
            whole,
            whole,
            own,
            pl.BlockSpec((group, pos_count, seq_len), lambda s, g: (g, 0, 0)),
            pl.BlockSpec((pos_count, seq_len), lambda s, g: (0, 0)),
            stat,
        ],
        out_specs=[
            own,
            stat,
            pl.BlockSpec((1, group, pos_count, seq_len), lambda s, g: (s, g, 0, 0)),
        ],
        out_shape=[
            jax.ShapeDtypeStruct(queries.shape, jnp.bfloat16),
            jax.ShapeDtypeStruct((seq_count, groups, pos_count, group), jnp.float32),
            jax.ShapeDtypeStruct(
                (seq_count, groups * group, pos_count, seq_len), jnp.bfloat16
            ),
        ],
        compiler_params=pltpu.CompilerParams(vmem_limit_bytes=48 * 2**20),
    )(queries, keys, values, grads, bias, seen, totals)


def attend_back_keys(keys, values, queries, grads, bias, seen, totals, dots, width, scale):
    seq_count, pos_count, model_width = keys.shape
    seq_len = queries.shape[1]
    block = 128
    group = block // width
    groups = model_width // block

    def kernel(
        k_ref, v_ref, q_ref, g_ref, bias_ref, seen_ref, total_ref, dot_ref, key_ref, value_ref
    ):
        for h in range(group):
            cut = slice(h * width, (h + 1) * width)
            scores = lanes_dot(k_ref[0, :, cut], q_ref[0, :, cut]) * scale + bias_ref[h]
            scores = jnp.where(seen_ref[...] > 0.0, scores, -1e30)
            attention = jnp.exp(scores - total_ref[0, 0, h : h + 1, :])
            prob_grad = lanes_dot(v_ref[0, :, cut], g_ref[0, :, cut])
            score_grad = (attention * (prob_grad - dot_ref[0, 0, h : h + 1, :])).astype(
                jnp.bfloat16
            )
            key_back = jnp.dot(score_grad, q_ref[0, :, cut], preferred_element_type=jnp.float32)
            key_ref[0, :, cut] = (key_back * scale).astype(jnp.bfloat16)
            value_ref[0, :, cut] = jnp.dot(
                attention.astype(jnp.bfloat16),
                g_ref[0, :, cut],
                preferred_element_type=jnp.float32,
            ).astype(jnp.bfloat16)

    own = pl.BlockSpec((1, pos_count, block), lambda s, g: (s, 0, g))
    whole = pl.BlockSpec((1, seq_len, block), lambda s, g: (s, 0, g))
    stat = pl.BlockSpec((1, 1, group, seq_len), lambda s, g: (s, g, 0, 0))
    return pl.pallas_call(
        kernel,
        grid=(seq_count, groups),
        in_specs=[
            own,
            own,
            whole,
            whole,
            pl.BlockSpec((group, pos_count, seq_len), lambda s, g: (g, 0, 0)),
            pl.BlockSpec((pos_count, seq_len), lambda s, g: (0, 0)),
            stat,
            stat,
        ],
        out_specs=[own, own],
        out_shape=[jax.ShapeDtypeStruct(keys.shape, jnp.bfloat16)] * 2,
        compiler_params=pltpu.CompilerParams(vmem_limit_bytes=48 * 2**20),
    )(keys, values, queries, grads, bias, seen, totals, dots)


def per_device(
    inputs,
    cotangent,
    expert_ids,
    first_gain,
    query_weight,
    key_weight,
    value_weight,
    merge_weight,
    relative_bucket_bias,
    expert_norm_gain,
    router_weight,
    gate_weight,
    up_weight,
    down_weight,
):
    seq_count, pos_count, model_width = inputs.shape
    bucket_num, heads_num = relative_bucket_bias.shape
    head_dimension = model_width // heads_num
    score_scale = head_dimension ** (-0.5)
    expert_num = router_weight.shape[1]
    local_experts = gate_weight.shape[0]
    owners = lax.axis_size("expert")
    places = lax.axis_size(("ctx", "dp"))
    seq_len = pos_count * places
    capacity = min(pos_count, max(2, 9 * pos_count // (4 * expert_num)))
    lane_rows = seq_count * capacity
    line_order, other_order = doubling_orders()
    row_order = [bit for bit in range(1, lax.axis_size("ctx").bit_length() - 1)] + [0]
    column_count = model_width // owners
    first_expert = lax.axis_index("expert") * local_experts
    residual = inputs.astype(jnp.float32)
    first_normed, first_back = jax.vjp(rms_scale, residual, first_gain)
    mixer_in = first_normed.astype(jnp.bfloat16)
    keys_local = jnp.einsum(
        "spd,de->spe", mixer_in, key_weight, preferred_element_type=jnp.float32
    ).astype(jnp.bfloat16)
    values_local = jnp.einsum(
        "spd,de->spe", mixer_in, value_weight, preferred_element_type=jnp.float32
    ).astype(jnp.bfloat16)
    keys_whole, values_whole = (
        whole.transpose(1, 0, 2, 3).reshape(seq_count, seq_len, model_width)
        for whole in doubling_gather(
            (keys_local, values_local), ("ctx", "dp"), (line_order, other_order), 1
        )
    )
    id_zeros = jnp.zeros((seq_count, pos_count, 126), jnp.bfloat16)
    cotangent_free, values_whole = lax.optimization_barrier((cotangent, values_whole))
    cotangent_all = lax.all_gather(
        jnp.concatenate([cotangent_free, expert_ids.astype(jnp.bfloat16), id_zeros], axis=-1),
        ("ctx", "expert"),
        axis=0,
        tiled=True,
    )
    ids_all = cotangent_all[..., model_width : model_width + 2].astype(jnp.int32)
    block_num = ids_all.shape[0]
    queries = jnp.einsum(
        "spd,de->spe", mixer_in, query_weight, preferred_element_type=jnp.float32
    ).astype(jnp.bfloat16)
    first_pos = lax.axis_index(("ctx", "dp")) * pos_count
    query_pos = first_pos + lax.iota(jnp.int32, pos_count)
    offsets = query_pos[:, None] - lax.iota(jnp.int32, seq_len)[None, :]
    distance = jnp.clip(offsets, 0, seq_len - 1)
    visible = (offsets >= 0).astype(jnp.float32)
    bias_lattice = bias_grid(relative_bucket_bias, distance)
    mixed_heads, total_cols = attend(
        queries, keys_whole, values_whole, bias_lattice, visible, head_dimension, score_scale
    )
    total_rows = total_cols.transpose(0, 2, 1, 3).reshape(seq_count, pos_count, heads_num)
    stat_pad = -(-3 * heads_num // 128) * 128 - 3 * heads_num
    stat_zeros = jnp.zeros((seq_count, pos_count, stat_pad), jnp.bfloat16)
    query_packed = jnp.concatenate([queries, *split_parts(total_rows, 3), stat_zeros], axis=-1)
    mixer_all = gather_back(mixer_in, "expert")
    hidden_state = residual + jnp.einsum(
        "spd,de->spe", mixed_heads, merge_weight, preferred_element_type=jnp.float32
    )
    second_normed, second_back = jax.vjp(rms_scale, hidden_state, expert_norm_gain)
    expert_input = second_normed.astype(jnp.bfloat16)
    own_hits = jnp.any(
        expert_ids[None] == lax.iota(jnp.int32, expert_num)[:, None, None, None], axis=-1
    )
    own_hot = slot_hot(own_hits, capacity)
    dispatched = (
        jnp.einsum("eskp,spd->eskd", own_hot, expert_input, preferred_element_type=jnp.float32)
        .astype(jnp.bfloat16)
        .reshape(owners, local_experts, lane_rows, model_width)
    )
    arrived = exchange((dispatched,), ("expert",), 2)[0]
    slot_rows = arrived.transpose(1, 0, 2, 3).reshape(
        local_experts, owners * lane_rows, model_width
    )
    (rows_whole,) = doubling_gather((slot_rows,), ("ctx",), (row_order,), 3)
    all_rows = rows_whole.transpose(1, 0, 2, 3).reshape(
        local_experts, block_num * capacity, model_width
    )
    my_experts = first_expert + lax.iota(jnp.int32, local_experts)
    block_hits = jnp.any(ids_all[None] == my_experts[:, None, None, None], axis=-1)
    block_hot = slot_hot(block_hits, capacity)
    other_ids = jnp.sum(ids_all, axis=-1)[None] - my_experts[:, None, None]
    row_other = jnp.sum(
        block_hot.astype(jnp.float32) * other_ids[:, :, None, :].astype(jnp.float32), axis=-1
    ).astype(jnp.int32).reshape(local_experts, block_num * capacity)
    cotangent_rows = jnp.einsum(
        "lbkp,bpd->lbkd", block_hot, cotangent_all[..., :model_width], preferred_element_type=jnp.float32
    ).astype(jnp.bfloat16).reshape(local_experts, block_num * capacity, model_width)
    row_logits = jnp.einsum(
        "lrd,de->lre", all_rows, router_weight, preferred_element_type=jnp.float32
    )
    expert_line = lax.iota(jnp.int32, expert_num)[None, None, :]
    own_logit = jnp.sum(
        jnp.where(expert_line == my_experts[:, None, None], row_logits, 0.0), axis=-1
    )
    other_logit = jnp.sum(jnp.where(expert_line == row_other[..., None], row_logits, 0.0), axis=-1)
    row_gates = jax.nn.sigmoid(own_logit - other_logit)
    all_grads = (row_gates[..., None] * cotangent_rows.astype(jnp.float32)).astype(jnp.bfloat16)
    gate_pre = jnp.einsum("erd,edf->erf", all_rows, gate_weight, preferred_element_type=jnp.float32)
    up_pre = jnp.einsum("erd,edf->erf", all_rows, up_weight, preferred_element_type=jnp.float32)
    hidden_float, act_back = jax.vjp(gated_hidden, gate_pre, up_pre)
    hidden_act = hidden_float.astype(jnp.bfloat16)
    partial_value = jnp.einsum(
        "erf,efd->erd", hidden_act, down_weight, preferred_element_type=jnp.float32
    ).astype(jnp.bfloat16)
    partial_value, all_grads = lax.optimization_barrier((partial_value, all_grads))
    expert_result = lax.psum_scatter(partial_value, "ctx", scatter_dimension=1, tiled=True)
    returning = expert_result.reshape(local_experts, owners, lane_rows, model_width).transpose(
        1, 0, 2, 3
    )
    hidden_grad = jnp.einsum(
        "erd,efd->erf", all_grads, down_weight, preferred_element_type=jnp.float32
    )
    gate_delta, up_delta = act_back(hidden_grad)
    gate_low = gate_delta.astype(jnp.bfloat16)
    up_low = up_delta.astype(jnp.bfloat16)
    row_part = (
        jnp.einsum("erf,edf->erd", gate_low, gate_weight, preferred_element_type=jnp.float32)
        + jnp.einsum("erf,edf->erd", up_low, up_weight, preferred_element_type=jnp.float32)
    ).astype(jnp.bfloat16)
    row_blocks = row_part.reshape(local_experts, -1, owners * lane_rows, model_width)
    (row_landed,) = exchange((row_blocks.transpose(1, 0, 2, 3),), ("ctx",), 4)
    row_grads = jnp.sum(row_landed.astype(jnp.float32), axis=0).astype(jnp.bfloat16)
    back_rows = row_grads.reshape(local_experts, owners, lane_rows, model_width).transpose(
        1, 0, 2, 3
    )
    returned, returned_grads = exchange((returning, back_rows), ("expert",), 5)
    mixed_all = gather_back(mixed_heads, "expert")
    query_whole = lax.all_gather(query_packed, ("ctx", "dp"), axis=1, tiled=True)
    down_part = jnp.einsum(
        "erf,erd->efd", hidden_act, all_grads, preferred_element_type=jnp.float32
    )
    gate_part = jnp.einsum("erd,erf->edf", all_rows, gate_low, preferred_element_type=jnp.float32)
    up_part = jnp.einsum("erd,erf->edf", all_rows, up_low, preferred_element_type=jnp.float32)
    gate_grad, up_grad, down_grad = (
        lax.psum_scatter(
            gate_part.astype(jnp.bfloat16), "dp", scatter_dimension=1, tiled=True
        ).astype(jnp.float32),
        lax.psum_scatter(
            up_part.astype(jnp.bfloat16), "dp", scatter_dimension=1, tiled=True
        ).astype(jnp.float32),
        lax.psum_scatter(
            down_part.astype(jnp.bfloat16), "dp", scatter_dimension=2, tiled=True
        ).astype(jnp.float32),
    )
    logits = jnp.einsum(
        "spd,de->spe", expert_input, router_weight, preferred_element_type=jnp.float32
    )
    pick_hot = expert_ids[..., None] == lax.iota(jnp.int32, expert_num)
    picked_logits = jnp.sum(jnp.where(pick_hot, logits[:, :, None, :], 0.0), axis=-1)
    gate_values, gate_back = jax.vjp(pair_softmax, picked_logits)
    upstream = cotangent.astype(jnp.float32)
    slot_table = own_hot.transpose(1, 0, 2, 3)
    choose = (
        slot_table[:, None] * pick_hot.transpose(0, 2, 3, 1)[:, :, :, None, :].astype(jnp.bfloat16)
    ).reshape(seq_count, 2, expert_num * capacity, pos_count)
    returned_rows = returned.reshape(expert_num, seq_count, capacity, model_width).transpose(
        1, 0, 2, 3
    ).reshape(seq_count, expert_num * capacity, model_width)
    picked = jnp.einsum(
        "sjmp,smd->sjpd", choose, returned_rows, preferred_element_type=jnp.float32
    )
    expert_sum = (
        gate_values[:, :, 0, None] * picked[:, 0] + gate_values[:, :, 1, None] * picked[:, 1]
    )
    layer_output = (hidden_state + expert_sum).astype(jnp.bfloat16)
    pair_delta = jnp.sum(upstream[:, None] * picked, axis=-1).transpose(0, 2, 1)
    (pick_grad,) = gate_back(pair_delta)
    logit_grad = jnp.sum(jnp.where(pick_hot, pick_grad[..., None], 0.0), axis=2).astype(
        jnp.bfloat16
    )
    router_part = jnp.einsum(
        "spe,spd->ed", logit_grad, expert_input, preferred_element_type=jnp.float32
    )
    expert_delta = jnp.einsum(
        "spe,de->spd", logit_grad, router_weight, preferred_element_type=jnp.float32
    )
    grad_rows = returned_grads.reshape(expert_num, seq_count, capacity, model_width).transpose(
        1, 0, 2, 3
    ).reshape(seq_count, expert_num * capacity, model_width)
    expert_delta = expert_delta + jnp.einsum(
        "smp,smd->spd",
        slot_table.reshape(seq_count, expert_num * capacity, pos_count),
        grad_rows,
        preferred_element_type=jnp.float32,
    )
    state_part, second_part = second_back(expert_delta)
    state_grad = state_part + upstream
    state_low = state_grad.astype(jnp.bfloat16)
    mixed_flat = jnp.einsum(
        "spe,de->spd", state_low, merge_weight, preferred_element_type=jnp.float32
    ).astype(jnp.bfloat16)
    query_back, dot_cols, score_grad = attend_back_queries(
        queries,
        keys_whole,
        values_whole,
        mixed_flat,
        bias_lattice,
        visible,
        total_cols,
        head_dimension,
        score_scale,
    )
    dot_rows = dot_cols.transpose(0, 2, 1, 3).reshape(seq_count, pos_count, heads_num)
    grad_packed = jnp.concatenate([mixed_flat, *split_parts(dot_rows, 3), stat_zeros], axis=-1)
    (grad_gathered,) = doubling_gather(
        (grad_packed,), ("ctx", "dp"), (line_order, other_order), 6
    )
    grad_whole = grad_gathered.transpose(1, 0, 2, 3).reshape(seq_count, seq_len, -1)

    def columns_of(value):
        return value.reshape(seq_count, pos_count, owners, column_count).transpose(2, 0, 1, 3)

    bias_portion = jnp.einsum(
        "stey,aey->at",
        score_grad,
        bucket_table(distance, bucket_num).astype(jnp.bfloat16),
        preferred_element_type=jnp.float32,
    )
    def stat_lines(packed):
        stat = packed[..., model_width:].astype(jnp.float32)
        joined = (
            stat[..., :heads_num]
            + stat[..., heads_num : 2 * heads_num]
            + stat[..., 2 * heads_num : 3 * heads_num]
        )
        return joined.transpose(0, 2, 1).reshape(seq_count, -1, 128 // head_dimension, seq_len)

    gap = lax.iota(jnp.int32, seq_len)[None, :] - query_pos[:, None]
    key_back, value_back = attend_back_keys(
        keys_local,
        values_local,
        query_whole,
        grad_whole,
        bias_grid(relative_bucket_bias, jnp.clip(gap, 0, seq_len - 1)),
        (gap >= 0).astype(jnp.float32),
        stat_lines(query_whole),
        stat_lines(grad_whole),
        head_dimension,
        score_scale,
    )
    merge_part = jnp.einsum(
        "ospd,ospc->dc",
        mixed_all,
        exchange_back(columns_of(state_low), "expert"),
        preferred_element_type=jnp.float32,
    )
    back_cut = jnp.stack(
        [columns_of(part) for part in (query_back, key_back, value_back)], axis=1
    )
    (back_all,) = exchange((back_cut,), ("expert",), 7, by_place=False)
    back_part = jnp.einsum(
        "ospd,onspc->dnc", mixer_all, back_all, preferred_element_type=jnp.float32
    ).reshape(model_width, 3 * column_count)
    dense_part = jnp.concatenate([back_part, merge_part], axis=1).astype(jnp.bfloat16)
    (dense_landed,) = exchange(
        (dense_part.reshape(places, model_width // places, 4 * column_count),), ("ctx", "dp"), 8
    )
    back_sum = jnp.sum(dense_landed.astype(jnp.float32), axis=0)
    mixer_delta = jnp.einsum(
        "spe,de->spd", query_back, query_weight, preferred_element_type=jnp.float32
    )
    mixer_delta = mixer_delta + jnp.einsum(
        "spe,de->spd", key_back, key_weight, preferred_element_type=jnp.float32
    )
    mixer_delta = mixer_delta + jnp.einsum(
        "spe,de->spd", value_back, value_weight, preferred_element_type=jnp.float32
    )
    input_part, first_part = first_back(mixer_delta)
    input_grad = state_grad + input_part
    first_sum, second_sum, router_sum, bias_total = total_over(
        (first_part, second_part, router_part, bias_portion), 9
    )
    return (
        layer_output,
        input_grad,
        first_sum,
        back_sum[:, :column_count],
        back_sum[:, column_count : 2 * column_count],
        back_sum[:, 2 * column_count : 3 * column_count],
        back_sum[:, 3 * column_count :],
        bias_total,
        second_sum,
        router_sum.T,
        gate_grad,
        up_grad,
        down_grad,
    )


def solution(mesh):
    in_specs = (
        P("expert", ("ctx", "dp"), None),
        P("expert", ("ctx", "dp"), None),
        P("expert", ("ctx", "dp"), None),
        P(),
        P(),
        P(),
        P(),
        P(),
        P(),
        P(),
        P(),
        P("expert", None, "ctx"),
        P("expert", None, "ctx"),
        P("expert", "ctx", None),
    )
    out_specs = (
        P("expert", ("ctx", "dp"), None),
        P("expert", ("ctx", "dp"), None),
        P(),
        P(("ctx", "dp"), "expert"),
        P(("ctx", "dp"), "expert"),
        P(("ctx", "dp"), "expert"),
        P(("ctx", "dp"), "expert"),
        P(),
        P(),
        P(),
        P("expert", "dp", "ctx"),
        P("expert", "dp", "ctx"),
        P("expert", "ctx", "dp"),
    )
    return jax.shard_map(
        per_device, mesh=mesh, in_specs=in_specs, out_specs=out_specs, check_vma=False
    )
```

```python
import math

import jax
import jax.numpy as jnp
from jax import lax
from jax.experimental import pallas as pl
from jax.experimental.pallas import tpu as pltpu
from jax.sharding import PartitionSpec as P

norm_eps = 1e-06
reach_span = 128.0


def bucket_bounds(bucket_num):
    exact_span = bucket_num // 2
    bounds = list(range(1, exact_span))
    for target in range(exact_span, bucket_num):
        border = exact_span
        while (
            exact_span
            + int(math.log(border / exact_span) / math.log(reach_span / exact_span) * exact_span)
            < target
        ):
            border += 1
        bounds.append(border)
    return bounds


def distance_buckets(distance, bucket_num):
    counted = jnp.zeros(distance.shape, jnp.int32)
    for border in bucket_bounds(bucket_num):
        counted = counted + (distance >= border).astype(jnp.int32)
    return counted


def rms_scale(values, gain_vec):
    return (
        values * lax.rsqrt(jnp.mean(values * values, axis=-1, keepdims=True) + norm_eps) * gain_vec
    )


def gated_hidden(gate_pre, up_pre):
    return 0.5 * gate_pre * (1.0 + lax.erf(gate_pre * math.sqrt(0.5))) * up_pre


def pair_softmax(logit_pair):
    return jax.nn.softmax(logit_pair, axis=-1)


def bucket_table(distance, bucket_num):
    bucket_of = distance_buckets(distance, bucket_num)
    return (lax.iota(jnp.int32, bucket_num)[:, None, None] == bucket_of[None]).astype(jnp.float32)


def split_parts(values, count):
    parts = []
    rest = values
    for _ in range(count):
        part = rest.astype(jnp.bfloat16)
        parts.append(part)
        rest = rest - part.astype(jnp.float32)
    return parts


def bias_line(bias_table, distance):
    values = jnp.einsum(
        "ry,rm->ym",
        bias_table,
        bucket_table(jnp.maximum(distance, 0)[None], bias_table.shape[0])[:, 0],
        precision=lax.Precision.HIGHEST,
    )
    return jnp.where(distance >= 0, values, -1e30)


def sheared(line, rows, columns):
    grid = jnp.broadcast_to(line, (rows, line.shape[-1]))
    return pltpu.roll(grid, 0, 1, stride=1, stride_axis=0)[:, :columns]


def slot_hot(hits, capacity):
    pos_count = hits.shape[-1]
    before = (
        lax.iota(jnp.int32, pos_count)[:, None] < lax.iota(jnp.int32, pos_count)[None, :]
    ).astype(jnp.bfloat16)
    slots = jnp.einsum(
        "...p,pq->...q", hits.astype(jnp.bfloat16), before, preferred_element_type=jnp.float32
    ).astype(jnp.int32)
    rows = lax.iota(jnp.int32, capacity)[:, None]
    return jnp.where(
        hits[..., None, :] & (slots[..., None, :] == rows), 1.0, 0.0
    ).astype(jnp.bfloat16)


def flat_place(axes):
    place = 0
    for axis in axes:
        place = place * lax.axis_size(axis) + lax.axis_index(axis)
    return place


def device_at(axes, place):
    coordinates = {}
    for axis in reversed(axes):
        size = lax.axis_size(axis)
        coordinates[axis] = lax.rem(place, size)
        place = place // size
    return coordinates


def greet(axes, peers):
    barrier = pltpu.get_barrier_semaphore()
    for peer in peers:
        pl.semaphore_signal(
            barrier, inc=1, device_id=device_at(axes, peer), device_id_type=pl.DeviceIdType.MESH
        )
    pl.semaphore_wait(barrier, len(peers))


def exchange(arrays, axes, collective_id, by_place=True):
    count = lax.axis_size(axes)
    num = len(arrays)

    def kernel(*refs):
        sources, targets = refs[:num], refs[num : 2 * num]
        own_sem, send_sem, recv_sem = refs[2 * num :]
        me = flat_place(axes)
        peers = [lax.rem(me + step, count) for step in range(1, count)]
        owns = []
        for k in range(num):
            own = pltpu.make_async_copy(sources[k].at[me], targets[k].at[me if by_place else 0], own_sem.at[k])
            own.start()
            owns.append(own)
        greet(axes, peers)
        copies = []
        for step, peer in enumerate(peers):
            for k in range(num):
                copy = pltpu.make_async_remote_copy(
                    src_ref=sources[k].at[peer],
                    dst_ref=targets[k].at[me if by_place else step + 1],
                    send_sem=send_sem.at[k, step],
                    recv_sem=recv_sem.at[k, step],
                    device_id=device_at(axes, peer),
                    device_id_type=pl.DeviceIdType.MESH,
                )
                copy.start()
                copies.append(copy)
        for copy in copies + owns:
            copy.wait()

    return pl.pallas_call(
        kernel,
        out_shape=[jax.ShapeDtypeStruct(array.shape, array.dtype) for array in arrays],
        in_specs=[pl.BlockSpec(memory_space=pl.ANY)] * num,
        out_specs=[pl.BlockSpec(memory_space=pl.ANY)] * num,
        scratch_shapes=[
            pltpu.SemaphoreType.DMA((num,)),
            pltpu.SemaphoreType.DMA((num, count - 1)),
            pltpu.SemaphoreType.DMA((num, count - 1)),
        ],
        compiler_params=pltpu.CompilerParams(collective_id=collective_id, has_side_effects=True),
    )(*arrays)


def flip(place, bit):
    return place + bit - 2 * bit * lax.rem(place // bit, 2)


def doubling_gather(arrays, axes, orders, collective_id):
    count = lax.axis_size(axes)
    num = len(arrays)
    stages = len(orders[0])
    pieces = []
    for k in range(num):
        rows = arrays[k].shape[1] // len(orders)
        pieces += [(k, n * rows, rows, order) for n, order in enumerate(orders)]

    def kernel(*refs):
        sources, targets = refs[:num], refs[num : 2 * num]
        own_sem, send_sem, recv_sem = refs[2 * num :]
        me = flat_place(axes)
        owns = []
        for k in range(num):
            own = pltpu.make_async_copy(sources[k], targets[k].at[me], own_sem.at[k])
            own.start()
            owns.append(own)
        greet(axes, [flip(me, 2**bit) for bit in range(stages)])
        held = [[me] for _ in pieces]
        for stage in range(stages):
            copies = []
            for p, (k, start, rows, order) in enumerate(pieces):
                bit = 2 ** order[stage]
                partner = device_at(axes, flip(me, bit))
                span = pl.ds(start, rows)
                for slot, block in enumerate(held[p]):
                    lane = 2**stage - 1 + slot
                    target = targets[k].at[block, :, span]
                    copy = pltpu.make_async_remote_copy(
                        src_ref=sources[k].at[:, span] if stage == 0 else target,
                        dst_ref=target,
                        send_sem=send_sem.at[p, lane],
                        recv_sem=recv_sem.at[p, lane],
                        device_id=partner,
                        device_id_type=pl.DeviceIdType.MESH,
                    )
                    copy.start()
                    copies.append(copy)
                held[p] = held[p] + [flip(block, bit) for block in held[p]]
            if stage == 0:
                for own in owns:
                    own.wait()
            for copy in copies:
                copy.wait()

    return pl.pallas_call(
        kernel,
        out_shape=[jax.ShapeDtypeStruct((count, *array.shape), array.dtype) for array in arrays],
        in_specs=[pl.BlockSpec(memory_space=pl.ANY)] * num,
        out_specs=[pl.BlockSpec(memory_space=pl.ANY)] * num,
        scratch_shapes=[
            pltpu.SemaphoreType.DMA((num,)),
            pltpu.SemaphoreType.DMA((len(pieces), count - 1)),
            pltpu.SemaphoreType.DMA((len(pieces), count - 1)),
        ],
        compiler_params=pltpu.CompilerParams(collective_id=collective_id, has_side_effects=True),
    )(*arrays)


def doubling_orders():
    dp_bits = lax.axis_size("dp").bit_length() - 1
    ctx_bits = lax.axis_size("ctx").bit_length() - 1
    inner = list(range(dp_bits))
    outer = list(range(dp_bits + 1, dp_bits + ctx_bits))
    last = [dp_bits] if ctx_bits else []
    return inner + outer + last, outer + inner + last


def sum_everywhere(packed, phases, collective_id):
    counts = [lax.axis_size(axes) for axes in phases]
    rows, lanes = packed.shape

    def kernel(x_ref, out_ref, *scratch):
        barrier = pltpu.get_barrier_semaphore()
        peers = []
        for axes, count in zip(phases, counts):
            me = flat_place(axes)
            peers.append([lax.rem(me + step, count) for step in range(1, count)])
        for axes, group in zip(phases, peers):
            for peer in group:
                pl.semaphore_signal(
                    barrier,
                    inc=1,
                    device_id=device_at(axes, peer),
                    device_id_type=pl.DeviceIdType.MESH,
                )
        pl.semaphore_wait(barrier, sum(len(group) for group in peers))
        out_ref[...] = x_ref[...]
        for phase, axes in enumerate(phases):
            mine, landed, send_sem, recv_sem = scratch[4 * phase : 4 * phase + 4]
            mine[...] = out_ref[...]
            copies = []
            for step, peer in enumerate(peers[phase]):
                copy = pltpu.make_async_remote_copy(
                    src_ref=mine,
                    dst_ref=landed.at[step],
                    send_sem=send_sem.at[step],
                    recv_sem=recv_sem.at[step],
                    device_id=device_at(axes, peer),
                    device_id_type=pl.DeviceIdType.MESH,
                )
                copy.start()
                copies.append(copy)
            for step, copy in enumerate(copies):
                copy.wait()
                out_ref[...] += landed[step]

    scratch = []
    for count in counts:
        scratch += [
            pltpu.VMEM((rows, lanes), jnp.float32),
            pltpu.VMEM((count - 1, rows, lanes), jnp.float32),
            pltpu.SemaphoreType.DMA((count - 1,)),
            pltpu.SemaphoreType.DMA((count - 1,)),
        ]
    return pl.pallas_call(
        kernel,
        out_shape=jax.ShapeDtypeStruct(packed.shape, packed.dtype),
        in_specs=[pl.BlockSpec(memory_space=pltpu.VMEM)],
        out_specs=pl.BlockSpec(memory_space=pltpu.VMEM),
        scratch_shapes=scratch,
        compiler_params=pltpu.CompilerParams(collective_id=collective_id, has_side_effects=True),
    )(packed)


def total_over(values, collective_id):
    flat = jnp.concatenate([value.reshape(-1) for value in values])
    size = flat.shape[0]
    packed = jnp.pad(flat, (0, (-size) % 1024)).reshape(-1, 128)
    summed = sum_everywhere(packed, (("ctx", "dp"), ("expert",)), collective_id).reshape(-1)
    outs = []
    offset = 0
    for value in values:
        outs.append(summed[offset : offset + value.size].reshape(value.shape))
        offset += value.size
    return outs


def shifted(value, axis, step):
    size = lax.axis_size(axis)
    return lax.ppermute(value, axis, [(i, (i + step) % size) for i in range(size)])


def gather_back(value, axis):
    size = lax.axis_size(axis)
    return jnp.stack([value] + [shifted(value, axis, step) for step in range(1, size)])


def exchange_back(blocks, axis):
    size = lax.axis_size(axis)
    me = lax.axis_index(axis)
    parts = [lax.dynamic_index_in_dim(blocks, me, 0, keepdims=False)]
    for step in range(1, size):
        block = lax.dynamic_index_in_dim(blocks, lax.rem(me + step, size), 0, keepdims=False)
        parts.append(shifted(block, axis, step))
    return jnp.stack(parts)


def lanes_dot(a, b):
    return lax.dot_general(a, b, (((1,), (1,)), ((), ())), preferred_element_type=jnp.float32)


def attend(queries, keys, values, line, width, scale):
    seq_count, pos_count, model_width = queries.shape
    seq_len = keys.shape[1]
    block = 128
    group = block // width
    groups = model_width // block

    def kernel(q_ref, k_ref, v_ref, line_ref, mixed_ref, total_ref):
        for h in range(group):
            cut = slice(h * width, (h + 1) * width)
            scores = lanes_dot(q_ref[0, :, cut], k_ref[0, :, cut]) * scale
            scores = scores + sheared(line_ref[0, h : h + 1, :], pos_count, seq_len)
            top = jnp.max(scores, axis=-1, keepdims=True)
            terms = jnp.exp(scores - top)
            total = jnp.sum(terms, axis=-1, keepdims=True)
            attention = (terms * (1.0 / total)).astype(jnp.bfloat16)
            mixed = jnp.dot(attention, v_ref[0, :, cut], preferred_element_type=jnp.float32)
            mixed_ref[0, :, cut] = mixed.astype(jnp.bfloat16)
            total_ref[0, 0, :, h : h + 1] = top + jnp.log(total)

    own = pl.BlockSpec((1, pos_count, block), lambda s, g: (s, 0, g))
    whole = pl.BlockSpec((1, seq_len, block), lambda s, g: (s, 0, g))
    return pl.pallas_call(
        kernel,
        grid=(seq_count, groups),
        in_specs=[
            own,
            whole,
            whole,
            pl.BlockSpec((1, group, seq_len + pos_count), lambda s, g: (g, 0, 0)),
        ],
        out_specs=[own, pl.BlockSpec((1, 1, pos_count, group), lambda s, g: (s, g, 0, 0))],
        out_shape=[
            jax.ShapeDtypeStruct(queries.shape, jnp.bfloat16),
            jax.ShapeDtypeStruct((seq_count, groups, pos_count, group), jnp.float32),
        ],
        compiler_params=pltpu.CompilerParams(vmem_limit_bytes=48 * 2**20),
    )(queries, keys, values, line)


def attend_back_queries(queries, keys, values, grads, line, totals, width, scale):
    seq_count, pos_count, model_width = queries.shape
    seq_len = keys.shape[1]
    block = 128
    group = block // width
    groups = model_width // block

    def kernel(
        q_ref, k_ref, v_ref, g_ref, line_ref, total_ref, back_ref, dot_ref, score_ref
    ):
        for h in range(group):
            cut = slice(h * width, (h + 1) * width)
            scores = lanes_dot(q_ref[0, :, cut], k_ref[0, :, cut]) * scale
            scores = scores + sheared(line_ref[0, h : h + 1, :], pos_count, seq_len)
            attention = jnp.exp(scores - total_ref[0, 0, :, h : h + 1])
            prob_grad = lanes_dot(g_ref[0, :, cut], v_ref[0, :, cut])
            row_dot = jnp.sum(attention * prob_grad, axis=-1, keepdims=True)
            score_grad = (attention * (prob_grad - row_dot)).astype(jnp.bfloat16)
            back = jnp.dot(score_grad, k_ref[0, :, cut], preferred_element_type=jnp.float32)
            back_ref[0, :, cut] = (back * scale).astype(jnp.bfloat16)
            dot_ref[0, 0, :, h : h + 1] = row_dot
            score_ref[0, h] = score_grad

    own = pl.BlockSpec((1, pos_count, block), lambda s, g: (s, 0, g))
    whole = pl.BlockSpec((1, seq_len, block), lambda s, g: (s, 0, g))
    stat = pl.BlockSpec((1, 1, pos_count, group), lambda s, g: (s, g, 0, 0))
    return pl.pallas_call(
        kernel,
        grid=(seq_count, groups),
        in_specs=[
            own,
            whole,
            whole,
            own,
            pl.BlockSpec((1, group, seq_len + pos_count), lambda s, g: (g, 0, 0)),
            stat,
        ],
        out_specs=[
            own,
            stat,
            pl.BlockSpec((1, group, pos_count, seq_len), lambda s, g: (s, g, 0, 0)),
        ],
        out_shape=[
            jax.ShapeDtypeStruct(queries.shape, jnp.bfloat16),
            jax.ShapeDtypeStruct((seq_count, groups, pos_count, group), jnp.float32),
            jax.ShapeDtypeStruct(
                (seq_count, groups * group, pos_count, seq_len), jnp.bfloat16
            ),
        ],
        compiler_params=pltpu.CompilerParams(vmem_limit_bytes=48 * 2**20),
    )(queries, keys, values, grads, line, totals)


def attend_back_keys(keys, values, queries, grads, line, totals, dots, width, scale):
    seq_count, pos_count, model_width = keys.shape
    seq_len = queries.shape[1]
    block = 128
    group = block // width
    groups = model_width // block

    def kernel(
        k_ref, v_ref, q_ref, g_ref, line_ref, total_ref, dot_ref, key_ref, value_ref
    ):
        for h in range(group):
            cut = slice(h * width, (h + 1) * width)
            scores = lanes_dot(k_ref[0, :, cut], q_ref[0, :, cut]) * scale
            scores = scores + sheared(line_ref[0, h : h + 1, :], pos_count, seq_len)
            attention = jnp.exp(scores - total_ref[0, 0, h : h + 1, :])
            prob_grad = lanes_dot(v_ref[0, :, cut], g_ref[0, :, cut])
            score_grad = (attention * (prob_grad - dot_ref[0, 0, h : h + 1, :])).astype(
                jnp.bfloat16
            )
            key_back = jnp.dot(score_grad, q_ref[0, :, cut], preferred_element_type=jnp.float32)
            key_ref[0, :, cut] = (key_back * scale).astype(jnp.bfloat16)
            value_ref[0, :, cut] = jnp.dot(
                attention.astype(jnp.bfloat16),
                g_ref[0, :, cut],
                preferred_element_type=jnp.float32,
            ).astype(jnp.bfloat16)

    own = pl.BlockSpec((1, pos_count, block), lambda s, g: (s, 0, g))
    whole = pl.BlockSpec((1, seq_len, block), lambda s, g: (s, 0, g))
    stat = pl.BlockSpec((1, 1, group, seq_len), lambda s, g: (s, g, 0, 0))
    return pl.pallas_call(
        kernel,
        grid=(seq_count, groups),
        in_specs=[
            own,
            own,
            whole,
            whole,
            pl.BlockSpec((1, group, seq_len + pos_count), lambda s, g: (g, 0, 0)),
            stat,
            stat,
        ],
        out_specs=[own, own],
        out_shape=[jax.ShapeDtypeStruct(keys.shape, jnp.bfloat16)] * 2,
        compiler_params=pltpu.CompilerParams(vmem_limit_bytes=48 * 2**20),
    )(keys, values, queries, grads, line, totals, dots)


def per_device(
    inputs,
    cotangent,
    expert_ids,
    first_gain,
    query_weight,
    key_weight,
    value_weight,
    merge_weight,
    relative_bucket_bias,
    expert_norm_gain,
    router_weight,
    gate_weight,
    up_weight,
    down_weight,
):
    seq_count, pos_count, model_width = inputs.shape
    bucket_num, heads_num = relative_bucket_bias.shape
    head_dimension = model_width // heads_num
    score_scale = head_dimension ** (-0.5)
    expert_num = router_weight.shape[1]
    local_experts = gate_weight.shape[0]
    owners = lax.axis_size("expert")
    places = lax.axis_size(("ctx", "dp"))
    seq_len = pos_count * places
    capacity = min(pos_count, max(2, 9 * pos_count // (4 * expert_num)))
    lane_rows = seq_count * capacity
    line_order, other_order = doubling_orders()
    row_order = [bit for bit in range(1, lax.axis_size("ctx").bit_length() - 1)] + [0]
    column_count = model_width // owners
    first_expert = lax.axis_index("expert") * local_experts
    residual = inputs.astype(jnp.float32)
    first_normed, first_back = jax.vjp(rms_scale, residual, first_gain)
    mixer_in = first_normed.astype(jnp.bfloat16)
    keys_local = jnp.einsum(
        "spd,de->spe", mixer_in, key_weight, preferred_element_type=jnp.float32
    ).astype(jnp.bfloat16)
    values_local = jnp.einsum(
        "spd,de->spe", mixer_in, value_weight, preferred_element_type=jnp.float32
    ).astype(jnp.bfloat16)
    keys_whole, values_whole = (
        whole.transpose(1, 0, 2, 3).reshape(seq_count, seq_len, model_width)
        for whole in doubling_gather(
            (keys_local, values_local), ("ctx", "dp"), (line_order, other_order), 1
        )
    )
    id_zeros = jnp.zeros((seq_count, pos_count, 126), jnp.bfloat16)
    cotangent_free, values_whole = lax.optimization_barrier((cotangent, values_whole))
    cotangent_all = lax.all_gather(
        jnp.concatenate([cotangent_free, expert_ids.astype(jnp.bfloat16), id_zeros], axis=-1),
        ("ctx", "expert"),
        axis=0,
        tiled=True,
    )
    ids_all = cotangent_all[..., model_width : model_width + 2].astype(jnp.int32)
    block_num = ids_all.shape[0]
    queries = jnp.einsum(
        "spd,de->spe", mixer_in, query_weight, preferred_element_type=jnp.float32
    ).astype(jnp.bfloat16)
    first_pos = lax.axis_index(("ctx", "dp")) * pos_count
    query_pos = first_pos + lax.iota(jnp.int32, pos_count)
    offsets = query_pos[:, None] - lax.iota(jnp.int32, seq_len)[None, :]
    distance = jnp.clip(offsets, 0, seq_len - 1)
    line_index = lax.iota(jnp.int32, seq_len + pos_count)
    line_index = jnp.where(line_index < seq_len, line_index, line_index - seq_len - pos_count)
    line_shape = (-1, 128 // head_dimension, seq_len + pos_count)
    query_line = bias_line(relative_bucket_bias, first_pos - line_index).reshape(line_shape)
    key_line = bias_line(relative_bucket_bias, line_index - first_pos).reshape(line_shape)
    mixed_heads, total_cols = attend(
        queries, keys_whole, values_whole, query_line, head_dimension, score_scale
    )
    total_rows = total_cols.transpose(0, 2, 1, 3).reshape(seq_count, pos_count, heads_num)
    stat_pad = -(-3 * heads_num // 128) * 128 - 3 * heads_num
    stat_zeros = jnp.zeros((seq_count, pos_count, stat_pad), jnp.bfloat16)
    query_packed = jnp.concatenate([queries, *split_parts(total_rows, 3), stat_zeros], axis=-1)
    mixer_all = gather_back(mixer_in, "expert")
    hidden_state = residual + jnp.einsum(
        "spd,de->spe", mixed_heads, merge_weight, preferred_element_type=jnp.float32
    )
    second_normed, second_back = jax.vjp(rms_scale, hidden_state, expert_norm_gain)
    expert_input = second_normed.astype(jnp.bfloat16)
    own_hits = jnp.any(
        expert_ids[None] == lax.iota(jnp.int32, expert_num)[:, None, None, None], axis=-1
    )
    own_hot = slot_hot(own_hits, capacity)
    dispatched = (
        jnp.einsum("eskp,spd->eskd", own_hot, expert_input, preferred_element_type=jnp.float32)
        .astype(jnp.bfloat16)
        .reshape(owners, local_experts, lane_rows, model_width)
    )
    arrived = exchange((dispatched,), ("expert",), 2)[0]
    slot_rows = arrived.transpose(1, 0, 2, 3).reshape(
        local_experts, owners * lane_rows, model_width
    )
    (rows_whole,) = doubling_gather((slot_rows,), ("ctx",), (row_order,), 3)
    all_rows = rows_whole.transpose(1, 0, 2, 3).reshape(
        local_experts, block_num * capacity, model_width
    )
    my_experts = first_expert + lax.iota(jnp.int32, local_experts)
    block_hits = jnp.any(ids_all[None] == my_experts[:, None, None, None], axis=-1)
    block_hot = slot_hot(block_hits, capacity)
    other_ids = jnp.sum(ids_all, axis=-1)[None] - my_experts[:, None, None]
    row_other = jnp.sum(
        block_hot.astype(jnp.float32) * other_ids[:, :, None, :].astype(jnp.float32), axis=-1
    ).astype(jnp.int32).reshape(local_experts, block_num * capacity)
    cotangent_rows = jnp.einsum(
        "lbkp,bpd->lbkd", block_hot, cotangent_all[..., :model_width], preferred_element_type=jnp.float32
    ).astype(jnp.bfloat16).reshape(local_experts, block_num * capacity, model_width)
    row_logits = jnp.einsum(
        "lrd,de->lre", all_rows, router_weight, preferred_element_type=jnp.float32
    )
    expert_line = lax.iota(jnp.int32, expert_num)[None, None, :]
    own_logit = jnp.sum(
        jnp.where(expert_line == my_experts[:, None, None], row_logits, 0.0), axis=-1
    )
    other_logit = jnp.sum(jnp.where(expert_line == row_other[..., None], row_logits, 0.0), axis=-1)
    row_gates = jax.nn.sigmoid(own_logit - other_logit)
    all_grads = (row_gates[..., None] * cotangent_rows.astype(jnp.float32)).astype(jnp.bfloat16)
    gate_pre = jnp.einsum("erd,edf->erf", all_rows, gate_weight, preferred_element_type=jnp.float32)
    up_pre = jnp.einsum("erd,edf->erf", all_rows, up_weight, preferred_element_type=jnp.float32)
    hidden_float, act_back = jax.vjp(gated_hidden, gate_pre, up_pre)
    hidden_act = hidden_float.astype(jnp.bfloat16)
    partial_value = jnp.einsum(
        "erf,efd->erd", hidden_act, down_weight, preferred_element_type=jnp.float32
    ).astype(jnp.bfloat16)
    partial_value, all_grads = lax.optimization_barrier((partial_value, all_grads))
    expert_result = lax.psum_scatter(partial_value, "ctx", scatter_dimension=1, tiled=True)
    returning = expert_result.reshape(local_experts, owners, lane_rows, model_width).transpose(
        1, 0, 2, 3
    )
    hidden_grad = jnp.einsum(
        "erd,efd->erf", all_grads, down_weight, preferred_element_type=jnp.float32
    )
    gate_delta, up_delta = act_back(hidden_grad)
    gate_low = gate_delta.astype(jnp.bfloat16)
    up_low = up_delta.astype(jnp.bfloat16)
    row_part = (
        jnp.einsum("erf,edf->erd", gate_low, gate_weight, preferred_element_type=jnp.float32)
        + jnp.einsum("erf,edf->erd", up_low, up_weight, preferred_element_type=jnp.float32)
    ).astype(jnp.bfloat16)
    row_blocks = row_part.reshape(local_experts, -1, owners * lane_rows, model_width)
    (row_landed,) = exchange((row_blocks.transpose(1, 0, 2, 3),), ("ctx",), 4)
    row_grads = jnp.sum(row_landed.astype(jnp.float32), axis=0).astype(jnp.bfloat16)
    back_rows = row_grads.reshape(local_experts, owners, lane_rows, model_width).transpose(
        1, 0, 2, 3
    )
    returned, returned_grads = exchange((returning, back_rows), ("expert",), 5)
    mixed_all = gather_back(mixed_heads, "expert")
    query_whole = lax.all_gather(query_packed, ("ctx", "dp"), axis=1, tiled=True)
    down_part = jnp.einsum(
        "erd,erf->edf", all_grads, hidden_act, preferred_element_type=jnp.float32
    )
    gate_part = jnp.einsum("erd,erf->edf", all_rows, gate_low, preferred_element_type=jnp.float32)
    up_part = jnp.einsum("erd,erf->edf", all_rows, up_low, preferred_element_type=jnp.float32)
    gate_grad, up_grad, down_grad = (
        lax.psum_scatter(
            gate_part.astype(jnp.bfloat16), "dp", scatter_dimension=1, tiled=True
        ).astype(jnp.float32),
        lax.psum_scatter(
            up_part.astype(jnp.bfloat16), "dp", scatter_dimension=1, tiled=True
        ).astype(jnp.float32),
        lax.psum_scatter(
            down_part.astype(jnp.bfloat16), "dp", scatter_dimension=1, tiled=True
        )
        .astype(jnp.float32)
        .transpose(0, 2, 1),
    )
    logits = jnp.einsum(
        "spd,de->spe", expert_input, router_weight, preferred_element_type=jnp.float32
    )
    pick_hot = expert_ids[..., None] == lax.iota(jnp.int32, expert_num)
    picked_logits = jnp.sum(jnp.where(pick_hot, logits[:, :, None, :], 0.0), axis=-1)
    gate_values, gate_back = jax.vjp(pair_softmax, picked_logits)
    upstream = cotangent.astype(jnp.float32)
    slot_table = own_hot.transpose(1, 0, 2, 3)
    choose = (
        slot_table[:, None] * pick_hot.transpose(0, 2, 3, 1)[:, :, :, None, :].astype(jnp.bfloat16)
    ).reshape(seq_count, 2, expert_num * capacity, pos_count)
    returned_rows = returned.reshape(expert_num, seq_count, capacity, model_width).transpose(
        1, 0, 2, 3
    ).reshape(seq_count, expert_num * capacity, model_width)
    picked = jnp.einsum(
        "sjmp,smd->sjpd", choose, returned_rows, preferred_element_type=jnp.float32
    )
    expert_sum = (
        gate_values[:, :, 0, None] * picked[:, 0] + gate_values[:, :, 1, None] * picked[:, 1]
    )
    layer_output = (hidden_state + expert_sum).astype(jnp.bfloat16)
    pair_delta = jnp.sum(upstream[:, None] * picked, axis=-1).transpose(0, 2, 1)
    (pick_grad,) = gate_back(pair_delta)
    logit_grad = jnp.sum(jnp.where(pick_hot, pick_grad[..., None], 0.0), axis=2).astype(
        jnp.bfloat16
    )
    router_part = jnp.einsum(
        "spe,spd->ed", logit_grad, expert_input, preferred_element_type=jnp.float32
    )
    expert_delta = jnp.einsum(
        "spe,de->spd", logit_grad, router_weight, preferred_element_type=jnp.float32
    )
    grad_rows = returned_grads.reshape(expert_num, seq_count, capacity, model_width).transpose(
        1, 0, 2, 3
    ).reshape(seq_count, expert_num * capacity, model_width)
    expert_delta = expert_delta + jnp.einsum(
        "smp,smd->spd",
        slot_table.reshape(seq_count, expert_num * capacity, pos_count),
        grad_rows,
        preferred_element_type=jnp.float32,
    )
    state_part, second_part = second_back(expert_delta)
    state_grad = state_part + upstream
    state_low = state_grad.astype(jnp.bfloat16)
    mixed_flat = jnp.einsum(
        "spe,de->spd", state_low, merge_weight, preferred_element_type=jnp.float32
    ).astype(jnp.bfloat16)
    query_back, dot_cols, score_grad = attend_back_queries(
        queries,
        keys_whole,
        values_whole,
        mixed_flat,
        query_line,
        total_cols,
        head_dimension,
        score_scale,
    )
    dot_rows = dot_cols.transpose(0, 2, 1, 3).reshape(seq_count, pos_count, heads_num)
    grad_packed = jnp.concatenate([mixed_flat, *split_parts(dot_rows, 3), stat_zeros], axis=-1)
    (grad_gathered,) = doubling_gather(
        (grad_packed,), ("ctx", "dp"), (line_order, other_order), 6
    )
    grad_whole = grad_gathered.transpose(1, 0, 2, 3).reshape(seq_count, seq_len, -1)

    def columns_of(value):
        return value.reshape(seq_count, pos_count, owners, column_count).transpose(2, 0, 1, 3)

    bias_portion = jnp.einsum(
        "stey,aey->at",
        score_grad,
        bucket_table(distance, bucket_num).astype(jnp.bfloat16),
        preferred_element_type=jnp.float32,
    )
    def stat_lines(packed):
        stat = packed[..., model_width:].astype(jnp.float32)
        joined = (
            stat[..., :heads_num]
            + stat[..., heads_num : 2 * heads_num]
            + stat[..., 2 * heads_num : 3 * heads_num]
        )
        return joined.transpose(0, 2, 1).reshape(seq_count, -1, 128 // head_dimension, seq_len)

    key_back, value_back = attend_back_keys(
        keys_local,
        values_local,
        query_whole,
        grad_whole,
        key_line,
        stat_lines(query_whole),
        stat_lines(grad_whole),
        head_dimension,
        score_scale,
    )
    merge_part = jnp.einsum(
        "ospd,ospc->dc",
        mixed_all,
        exchange_back(columns_of(state_low), "expert"),
        preferred_element_type=jnp.float32,
    )
    back_cut = jnp.stack(
        [columns_of(part) for part in (query_back, key_back, value_back)], axis=1
    )
    (back_all,) = exchange((back_cut,), ("expert",), 7, by_place=False)
    back_part = jnp.einsum(
        "ospd,onspc->dnc", mixer_all, back_all, preferred_element_type=jnp.float32
    ).reshape(model_width, 3 * column_count)
    dense_part = jnp.concatenate([back_part, merge_part], axis=1).astype(jnp.bfloat16)
    (dense_landed,) = exchange(
        (dense_part.reshape(places, model_width // places, 4 * column_count),), ("ctx", "dp"), 8
    )
    back_sum = jnp.sum(dense_landed.astype(jnp.float32), axis=0)
    mixer_delta = jnp.einsum(
        "spe,de->spd", query_back, query_weight, preferred_element_type=jnp.float32
    )
    mixer_delta = mixer_delta + jnp.einsum(
        "spe,de->spd", key_back, key_weight, preferred_element_type=jnp.float32
    )
    mixer_delta = mixer_delta + jnp.einsum(
        "spe,de->spd", value_back, value_weight, preferred_element_type=jnp.float32
    )
    input_part, first_part = first_back(mixer_delta)
    input_grad = state_grad + input_part
    first_sum, second_sum, router_sum, bias_total = total_over(
        (first_part, second_part, router_part, bias_portion), 9
    )
    return (
        layer_output,
        input_grad,
        first_sum,
        back_sum[:, :column_count],
        back_sum[:, column_count : 2 * column_count],
        back_sum[:, 2 * column_count : 3 * column_count],
        back_sum[:, 3 * column_count :],
        bias_total,
        second_sum,
        router_sum.T,
        gate_grad,
        up_grad,
        down_grad,
    )


def solution(mesh):
    in_specs = (
        P("expert", ("ctx", "dp"), None),
        P("expert", ("ctx", "dp"), None),
        P("expert", ("ctx", "dp"), None),
        P(),
        P(),
        P(),
        P(),
        P(),
        P(),
        P(),
        P(),
        P("expert", None, "ctx"),
        P("expert", None, "ctx"),
        P("expert", "ctx", None),
    )
    out_specs = (
        P("expert", ("ctx", "dp"), None),
        P("expert", ("ctx", "dp"), None),
        P(),
        P(("ctx", "dp"), "expert"),
        P(("ctx", "dp"), "expert"),
        P(("ctx", "dp"), "expert"),
        P(("ctx", "dp"), "expert"),
        P(),
        P(),
        P(),
        P("expert", "dp", "ctx"),
        P("expert", "dp", "ctx"),
        P("expert", "ctx", "dp"),
    )
    return jax.shard_map(
        per_device, mesh=mesh, in_specs=in_specs, out_specs=out_specs, check_vma=False
    )
```
